256 devices in a mesh: group: 2 (over z_hi), seq: 16 (over z_lo, x), mp: 8 (over y, core).
Axes of the slice: x: 4, y: 4, z: 8 (z_hi: 2, z_lo: 4; z = z_hi * 4 + z_lo), core: 2. Of those that a mesh axis runs over, the one named last changes fastest.
Arguments:
- image_states: bfloat16 [16, 256, 7680], P('seq'), may hold values from -6 to 6
- norm_gain: float32 [1280], replicated, may hold values from 0.1 to 1.9
- proj_weight: bfloat16 [7680, 8192], P('seq', 'mp'), may hold values from -0.0625 to 0.0625
- kv_weight: bfloat16 [8192, 2048], P('mp'), may hold values from -0.0625 to 0.0625
- key_gain: float32 [128], replicated, may hold values from 0.1 to 1.9
- queries: bfloat16 [4096, 8192], P('seq', 'mp'), may hold values from -6 to 6
- query_gain: float32 [128], replicated, may hold values from 0.1 to 1.9
- head_gate: float32 [64], P('mp'), may hold values from 0.3 to 1.5
- cotangent: bfloat16 [4096, 8192], P('seq', 'mp'), may hold values from -192 to 192
- block_image: int32 [256, 1], P('seq'), may hold values from 0 to 15; in each aligned block of 16 rows (0 to 15, 16 to 31, ...) at most 2 rows name the same one
- image_len: int32 [16], replicated, may hold values from 64 to 256, as said below
Outputs:
- gradients: bfloat16 [2, 4096, 8192], P('group', 'seq', 'mp')
The draws below stay inside these ranges and needn't reach their ends.
Inputs may be any that keep to these rules, and one draw needn't show every extreme that they name: Text tokens b * 16 to (b + 1) * 16 - 1 attend the image block_image[b, 0]; within the 16 text blocks of one index of seq (aligned blocks of rows) no image is attended by more than 2 text blocks. Image i holds image_len[i] tokens; its key slots from image_len[i] on are left out.
All inputs are finite; a program needn't handle non-finite values.
Results may differ from the reference program's by a relative error of at most 0.013.
Values may be sent and summed in bfloat16 or wider, within the bound.
A program may use at most 128 MiB of HBM per device.

```python
import math
import jax
import jax.numpy as jnp
import numpy as np
from jax import lax

VIN = 7680
VD = 1280
DP = 8192
QH = 64
KVH = 8
HD = 128
IMG_TOK = 256
BLK = 16
MOST = 2
BLK_DEV = 16
IMAGES = 16
TEXT = 4096
NBLK = 256


def draw_image_len(key, part):
    key = jax.random.fold_in(key, 11)
    first_key, second_key = jax.random.split(key)
    counts = jax.random.randint(first_key, (IMAGES,), IMG_TOK // 4, IMG_TOK + 1)
    shuffle = jax.random.permutation(second_key, IMAGES)
    counts = counts.at[shuffle[0]].set(IMG_TOK)
    counts = counts.at[shuffle[1]].set(IMG_TOK // 4)
    return counts.astype(jnp.int32)


def level_of(rng, dims, shards, smallest, largest):
    def one(dim, parts):
        steps = jax.random.uniform(jax.random.fold_in(jax.random.fold_in(rng, 6), dim), (parts,), jnp.float32, smallest / len(shards), largest / len(shards))
        return jnp.repeat(jnp.exp(steps), dims[dim] // parts).reshape((-1,) + (1,) * (len(dims) - dim - 1))

    gain = one(*shards[0])
    for cut in shards[1:]:
        gain = gain * one(*cut)
    return gain


def assign_block(stream_key, own, number, rows, amount, top, reach, lean):
    sequence = jax.random.permutation(stream_key, amount)
    heavy_load, usual = shares(amount, rows * top, reach, lean, True), shares(amount, rows * top, reach, lean, False)
    places = jnp.arange(amount)

    def named(sizes, turn):
        used = int((sizes > 0).sum())
        fixed = max(1, used // 4)
        shifted = fixed + (places - fixed + turn * (used - fixed)) % max(1, amount - fixed)
        return jnp.zeros((amount,), jnp.int32).at[sequence[jnp.where(places < fixed, places, shifted)]].set(jnp.asarray(sizes, jnp.int32))

    sizes = jnp.where(number % 4 == 0, named(heavy_load, number // 4), named(usual, number - number // 4 - 1))
    mixed = jax.random.permutation(jax.random.fold_in(own, 3), amount)
    giver, receiver = mixed[0:amount // 2 * 2:2], mixed[1:amount // 2 * 2:2]
    room = jnp.minimum(sizes[giver] - 1, reach - sizes[receiver]) // 2
    room = jnp.where((giver == sequence[0]) | (receiver == sequence[0]) | (sizes[receiver] == 0), 0, jnp.maximum(room, 0))
    shifted = jax.random.randint(jax.random.fold_in(own, 4), (amount // 2,), 0, 1 << 20) % (room + 1)
    sizes = sizes.at[giver].add(-shifted).at[receiver].add(shifted)
    items = jnp.searchsorted(jnp.cumsum(sizes), jnp.arange(rows * top), side="right").astype(jnp.int32)
    table = items.reshape(top, rows).T
    table = table[jax.random.permutation(jax.random.fold_in(own, 1), rows)]
    turn = jax.random.randint(jax.random.fold_in(own, 2), (rows, 1), 0, top)
    return jnp.take_along_axis(table, (jnp.arange(top)[None, :] + turn) % top, axis=1)


def shares(amount, total, limit, slope, full):
    portions = [(1 << 20) // math.isqrt(rank ** slope) + 1 for rank in range(1, amount + 1)]
    largest = limit if full else min(limit, max(-(-total // amount), total * portions[0] // sum(portions)))
    least = 1 if total - largest >= amount - 1 else 0
    given, rest = [largest] + [least] * (amount - 1), total - largest - least * (amount - 1)
    while rest > 0:
        movable = [i for i in range(1, amount) if given[i] < largest] or [i for i in range(1, amount) if given[i] < limit]
        pool, budget = sum([portions[i] for i in movable]), rest
        for i in movable:
            addition = min(limit - given[i], max(1, budget * portions[i] // pool), rest)
            given[i] = given[i] + addition
            rest = rest - addition
    return np.array(given)


def centred(key, extent, scale, bound, cuts=(), kind=jnp.bfloat16):
    level = level_of(key, extent, cuts, -0.22, 0.18) if cuts else 1.0
    result = jax.random.normal(key, extent, jnp.float32) * scale * level
    return jnp.minimum(jnp.maximum(result, -bound), bound).astype(kind)


def setup_inputs(seed: int = 0) -> dict:
    arg_keys = jax.random.split(jax.random.key(seed), 12)
    image_states = centred(arg_keys[0], (IMAGES, IMG_TOK, VIN), 1.0, 6.0, ((0, 16),))
    norm_gain = jnp.clip(1.0 + 0.18 * jax.random.normal(arg_keys[1], (VD,), jnp.float32), 0.1, 1.9)
    proj_weight = centred(arg_keys[2], (VIN, DP), VIN ** -0.5, 0.0625, ((0, 16), (1, 8)))
    kv_weight = centred(arg_keys[3], (DP, KVH * 2 * HD), DP ** -0.5, 0.0625, ((0, 8),))
    key_gain = jnp.clip(1.0 + 0.18 * jax.random.normal(arg_keys[4], (HD,), jnp.float32), 0.1, 1.9)
    queries = centred(arg_keys[5], (TEXT, DP), 1.0, 6.0, ((0, 16), (1, 8)))
    query_gain = jnp.clip(1.0 + 0.18 * jax.random.normal(arg_keys[6], (HD,), jnp.float32), 0.1, 1.9)
    head_gate = jnp.clip(0.3 + 1.2 * jax.random.uniform(arg_keys[7], (QH,), jnp.float32) ** level_of(arg_keys[7], (QH,), ((0, 8),), -0.2, 0.2), 0.3, 1.5)
    cotangent = centred(arg_keys[8], (TEXT, DP), 32.0, 192.0, ((0, 16), (1, 8)))
    block_image_keys = jax.random.split(jax.random.fold_in(arg_keys[9], 1), NBLK // BLK_DEV)
    block_image_turns = jax.random.permutation(jax.random.fold_in(arg_keys[9], 3), NBLK // BLK_DEV)
    block_image = jax.vmap(lambda own, number: assign_block(jax.random.fold_in(arg_keys[9], 2), own, number, BLK_DEV, IMAGES, 1, MOST, 1))(block_image_keys, block_image_turns).reshape((NBLK, 1))
    image_len = draw_image_len(jax.random.fold_in(arg_keys[11], 71), 0)
    return dict(image_states=image_states, norm_gain=norm_gain, proj_weight=proj_weight, kv_weight=kv_weight, key_gain=key_gain, queries=queries, query_gain=query_gain, head_gate=head_gate, cotangent=cotangent, block_image=block_image, image_len=image_len)


epsilon = 1e-05

def root_scaled(values, scales):
    return values * lax.rsqrt(lax.optimization_barrier(jnp.mean(values * values, axis=-1, keepdims=True)) + epsilon) * scales

def reference(image_states, norm_gain, proj_weight, kv_weight, key_gain, queries, query_gain, head_gate, cotangent, block_image, image_len):
    flattened = image_states.reshape(IMAGES * IMG_TOK, VIN)
    leading = flattened[:, :VD].astype(jnp.float32)
    center = lax.optimization_barrier(jnp.mean(leading, axis=-1, keepdims=True))
    spread = lax.optimization_barrier(jnp.mean((leading - center) ** 2, axis=-1, keepdims=True))
    normed_lead = ((leading - center) * lax.rsqrt(spread + epsilon) * norm_gain).astype(jnp.bfloat16)
    normed = jnp.concatenate([normed_lead, flattened[:, VD:]], axis=1)
    features = jnp.dot(normed, proj_weight, preferred_element_type=jnp.float32).astype(jnp.bfloat16)
    projected = jnp.dot(features, kv_weight, preferred_element_type=jnp.float32).reshape(IMAGES * IMG_TOK, KVH, 2, HD)

    def key_normed(incoming):
        return root_scaled(incoming, key_gain)

    def query_normed(incoming):
        return root_scaled(incoming, query_gain)
    keys_out, key_back = jax.vjp(key_normed, projected[:, :, 0])
    keys = keys_out.astype(jnp.bfloat16).reshape(IMAGES, IMG_TOK, KVH, HD)
    values = projected[:, :, 1].astype(jnp.bfloat16).reshape(IMAGES, IMG_TOK, KVH, HD)
    group_size = QH // KVH
    query_wide = queries.astype(jnp.float32).reshape(TEXT, QH, HD)
    query_out, query_back = jax.vjp(query_normed, query_wide)
    query_low = query_out.astype(jnp.bfloat16).reshape(NBLK, BLK, KVH, group_size, HD)
    gate_values = jnp.tanh(head_gate).reshape(KVH, group_size)
    grad_low = (cotangent.astype(jnp.float32).reshape(NBLK, BLK, KVH, group_size, HD) * gate_values[None, None, :, :, None]).astype(jnp.bfloat16)
    chosen_image = block_image[:, 0]
    lengths = image_len[chosen_image]
    usable = (jnp.arange(IMG_TOK, dtype=jnp.int32)[None, :] < lengths[:, None]).astype(jnp.float32)
    membership = (jnp.arange(IMAGES, dtype=jnp.int32)[:, None] == chosen_image[None, :]).astype(jnp.float32)
    inverse_root = 1.0 / math.sqrt(HD)

    def one_group(packed):
        query_group, grad_group, key_group, value_group = packed
        chosen_keys = jnp.take(key_group, chosen_image, axis=0).astype(jnp.float32)
        chosen_values = jnp.take(value_group, chosen_image, axis=0).astype(jnp.float32)
        query_float = query_group.astype(jnp.float32)
        grad_float = grad_group.astype(jnp.float32)
        scores = jnp.einsum('btgd,bjd->bgtj', query_float, chosen_keys) * inverse_root
        raised = jnp.exp(scores) * usable[:, None, None, :]
        weights = raised / lax.optimization_barrier(jnp.sum(raised, axis=-1, keepdims=True))
        weights_low = weights.astype(jnp.bfloat16)
        weight_grads = jnp.einsum('btgd,bjd->bgtj', grad_float, chosen_values)
        row_inner = lax.optimization_barrier(jnp.sum(weights * weight_grads, axis=-1, keepdims=True))
        score_grads = (weights * (weight_grads - row_inner) * inverse_root).astype(jnp.bfloat16)
        query_grads = jnp.einsum('bgtj,bjd->btgd', score_grads.astype(jnp.float32), chosen_keys)
        key_blocks = jnp.einsum('bgtj,btgd->bjd', score_grads.astype(jnp.float32), query_float)
        value_blocks = jnp.einsum('bgtj,btgd->bjd', weights_low.astype(jnp.float32), grad_float)
        key_grads = jnp.dot(membership, key_blocks.reshape(NBLK, IMG_TOK * HD), precision=lax.Precision.HIGHEST, preferred_element_type=jnp.float32)
        value_grads = jnp.dot(membership, value_blocks.reshape(NBLK, IMG_TOK * HD), precision=lax.Precision.HIGHEST, preferred_element_type=jnp.float32)
        return (query_grads, key_grads.reshape(IMAGES, IMG_TOK, HD), value_grads.reshape(IMAGES, IMG_TOK, HD))
    query_grads, key_grads, value_grads = lax.map(one_group, (jnp.moveaxis(query_low, 2, 0), jnp.moveaxis(grad_low, 2, 0), jnp.moveaxis(keys, 2, 0), jnp.moveaxis(values, 2, 0)))
    query_grads = jnp.moveaxis(query_grads, 0, 2).reshape(TEXT, QH, HD)
    query_result = query_back(query_grads)[0].reshape(TEXT, DP).astype(jnp.bfloat16)
    key_grads = jnp.moveaxis(key_grads, 0, 2).reshape(IMAGES * IMG_TOK, KVH, HD)
    value_grads = jnp.moveaxis(value_grads, 0, 2).reshape(IMAGES * IMG_TOK, KVH, HD)
    key_raw_grads = key_back(key_grads)[0]
    projected_grads = jnp.stack([key_raw_grads, value_grads], axis=2).reshape(IMAGES * IMG_TOK, KVH * 2 * HD).astype(jnp.bfloat16)
    feature_grads = jnp.dot(projected_grads, kv_weight.T, preferred_element_type=jnp.float32).astype(jnp.bfloat16)
    return jnp.stack([feature_grads, query_result])
```

```python
import math

import jax
import jax.numpy as jnp
from jax import lax
from jax.sharding import PartitionSpec as P

epsilon = 1e-05


def passed_along(x, axis, by):
    length = lax.axis_size(axis)
    pairs = [(i, i + by) for i in range(length) if 0 <= i + by < length]
    return lax.ppermute(x, axis, pairs)


def root_scaled(values, scales):
    return values * lax.rsqrt(jnp.mean(values * values, axis=-1, keepdims=True) + epsilon) * scales


def per_device(
    image_states,
    norm_gain,
    proj_weight,
    kv_weight,
    key_gain,
    queries,
    query_gain,
    head_gate,
    cotangent,
    block_image,
    image_len,
):
    vision = lax.axis_index("group") == 0
    images_here, image_rows, input_width = image_states.shape
    norm_width = norm_gain.shape[0]
    own_rows = images_here * image_rows
    head_size = key_gain.shape[0]
    kv_width = kv_weight.shape[1] // lax.axis_size("mp")
    kv_here = kv_width // (2 * head_size)
    feature_cols = proj_weight.shape[1]
    image_count = image_len.shape[0]
    flattened = image_states.reshape(own_rows, input_width)
    leading = flattened[:, :norm_width].astype(jnp.float32)
    center = jnp.mean(leading, axis=-1, keepdims=True)
    spread = jnp.mean((leading - center) ** 2, axis=-1, keepdims=True)
    normed_lead = ((leading - center) * lax.rsqrt(spread + epsilon) * norm_gain).astype(
        jnp.bfloat16
    )
    normed = jnp.concatenate([normed_lead, flattened[:, norm_width:]], axis=1)
    portion = jnp.dot(proj_weight, kv_weight, preferred_element_type=jnp.float32)
    portion = lax.psum_scatter(
        portion.astype(jnp.bfloat16), "mp", scatter_dimension=1, tiled=True
    )
    portion = lax.all_gather(portion, "seq", axis=0, tiled=True)
    projected = jnp.dot(normed, portion, preferred_element_type=jnp.float32).reshape(
        own_rows, kv_here, 2, head_size
    )

    def key_normed(incoming):
        return root_scaled(incoming, key_gain)

    def query_normed(incoming):
        return root_scaled(incoming, query_gain)

    keys_out, key_back = jax.vjp(key_normed, projected[:, :, 0])
    keyval = jnp.stack(
        [keys_out.astype(jnp.bfloat16), projected[:, :, 1].astype(jnp.bfloat16)], axis=2
    ).reshape(images_here, image_rows, kv_width)
    tokens_here, column_count = queries.shape
    blocks = block_image.shape[0]
    block_rows = tokens_here // blocks
    heads_here = head_gate.shape[0]
    group_size = heads_here // kv_here
    inverse_root = 1.0 / math.sqrt(head_size)
    chosen_image = block_image[:, 0]
    query_blocks = queries.reshape(blocks, block_rows, column_count)
    cot_blocks = cotangent.reshape(blocks, block_rows, column_count)

    def lengths_of(image_ids):
        return jnp.sum(
            jnp.where(
                image_ids[:, None] == jnp.arange(image_count, dtype=jnp.int32)[None, :],
                image_len[None, :],
                0,
            ),
            axis=1,
        )

    def attend_core(query_rows, cot_rows, chosen, lengths):
        block_count = query_rows.shape[0]
        query_wide = query_rows.astype(jnp.float32).reshape(
            block_count * block_rows, heads_here, head_size
        )
        query_out, query_back = jax.vjp(query_normed, query_wide)
        query_low = query_out.astype(jnp.bfloat16).reshape(
            block_count, block_rows, kv_here, group_size, head_size
        )
        chosen = chosen.reshape(block_count, image_rows, kv_here, 2, head_size)
        chosen_keys = chosen[:, :, :, 0]
        chosen_values = chosen[:, :, :, 1]
        usable = (jnp.arange(image_rows, dtype=jnp.int32)[None, :] < lengths[:, None]).astype(
            jnp.float32
        )
        scores = (
            jnp.einsum(
                "btkgd,bjkd->bkgtj", query_low, chosen_keys, preferred_element_type=jnp.float32
            )
            * inverse_root
        )
        raised = jnp.exp(scores) * usable[:, None, None, None, :]
        weights = raised / jnp.sum(raised, axis=-1, keepdims=True)
        weights_low = weights.astype(jnp.bfloat16)
        gate_values = jnp.tanh(head_gate).reshape(kv_here, group_size)
        grad_low = (
            cot_rows.astype(jnp.float32).reshape(
                block_count, block_rows, kv_here, group_size, head_size
            )
            * gate_values[None, None, :, :, None]
        ).astype(jnp.bfloat16)
        weight_grads = jnp.einsum(
            "btkgd,bjkd->bkgtj", grad_low, chosen_values, preferred_element_type=jnp.float32
        )
        row_inner = jnp.sum(weights * weight_grads, axis=-1, keepdims=True)
        score_grads = (weights * (weight_grads - row_inner) * inverse_root).astype(jnp.bfloat16)
        query_grads = jnp.einsum(
            "bkgtj,bjkd->btkgd", score_grads, chosen_keys, preferred_element_type=jnp.float32
        ).reshape(block_count * block_rows, heads_here, head_size)
        query_result = (
            query_back(query_grads)[0]
            .reshape(block_count * block_rows, heads_here * head_size)
            .astype(jnp.bfloat16)
        )
        key_grads = jnp.einsum(
            "bkgtj,btkgd->bjkd", score_grads, query_low, preferred_element_type=jnp.float32
        )
        value_grads = jnp.einsum(
            "bkgtj,btkgd->bjkd", weights_low, grad_low, preferred_element_type=jnp.float32
        )
        block_grads = jnp.stack([key_grads, value_grads], axis=3).reshape(
            block_count, image_rows * kv_width
        )
        return (query_result, block_grads)

    gathered = lax.all_gather(keyval, "seq", axis=0, tiled=True)
    every_image = gathered

    def attend_all(images_all):
        chosen = jnp.take(images_all, chosen_image, axis=0)
        return attend_core(query_blocks, cot_blocks, chosen, lengths_of(chosen_image))

    def skipped_all(images_all):
        return (
            jnp.zeros((tokens_here, column_count), jnp.bfloat16),
            jnp.zeros((blocks, image_rows * kv_width), jnp.float32),
        )

    query_result, block_grads = lax.cond(vision, skipped_all, attend_all, every_image)
    image_ids = jnp.arange(lax.axis_size("seq") * own_rows // image_rows, dtype=jnp.int32)
    membership = (image_ids[:, None] == chosen_image[None, :]).astype(jnp.float32)
    summed = jnp.dot(
        membership, block_grads, precision=lax.Precision.HIGHEST, preferred_element_type=jnp.float32
    )
    own_sum = lax.psum_scatter(
        summed.reshape(lax.axis_size("seq") * own_rows, kv_width).astype(jnp.bfloat16),
        "seq",
        scatter_dimension=0,
        tiled=True,
    )
    returned = passed_along(own_sum, "group", -1)
    returned = returned.astype(jnp.float32).reshape(own_rows, kv_here, 2, head_size)
    key_raw_grads = key_back(returned[:, :, 0])[0]
    projected_grads = (
        jnp.stack([key_raw_grads, returned[:, :, 1]], axis=2)
        .reshape(own_rows, kv_width)
        .astype(jnp.bfloat16)
    )
    add_portion = lax.all_gather(projected_grads, "mp", axis=1, tiled=True)

    def accumulate(carried):
        return lax.dot_general(
            add_portion, kv_weight, (((1,), (1,)), ((), ())), preferred_element_type=jnp.float32
        )

    def unchanged(carried):
        return carried

    feature_grads = lax.cond(
        vision, accumulate, unchanged, jnp.zeros((own_rows, feature_cols), jnp.float32)
    ).astype(jnp.bfloat16)
    result = jnp.where(vision, feature_grads, query_result)
    return result[None]


def solution(mesh):
    placed = (
        P("seq", None, None),
        P(),
        P("seq", "mp"),
        P("mp", None),
        P(),
        P("seq", "mp"),
        P(),
        P("mp"),
        P("seq", "mp"),
        P("seq", None),
        P(),
    )
    return jax.shard_map(
        per_device, mesh=mesh, in_specs=placed, out_specs=P("group", "seq", "mp"), check_vma=False
    )
```

```python
import math

import jax
import jax.numpy as jnp
from jax import lax
from jax.experimental import pallas as pl
from jax.experimental.pallas import tpu as pltpu
from jax.sharding import PartitionSpec as P

MESH = pl.DeviceIdType.MESH
F32, BF16 = jnp.float32, jnp.bfloat16
epsilon = 1e-05

VIN, VD, HD = 7680, 1280, 128
ROWS = 256
WROWS = 480
WHALF = WROWS // 2
HALF = ROWS // 2
INV = 1.0 / math.sqrt(HD)

RIGHT, LEFT = 0, 1

_sizes = dict(
    wsib=2, wy=6, qg=1,
    wz=4, wzf=2, wx=16, wxf=8,
    kz=4, kzf=2, kx=16, kxf=8,
    share=16, gsib=16,
    rxo=8, rx=16, rzo=2, rz=4,
    pgx=1, pgy=6, pgs=2, dq=2,
)
BASE = {}
_total = 0
for _name, _size in _sizes.items():
    BASE[_name] = _total
    _total += _size
PLACES = _total


def gray(k):
    return k + (k // 2) * (1 - 2 * (k % 2))


def nt(a, b):
    return lax.dot_general(a, b, (((1,), (1,)), ((), ())), preferred_element_type=F32)


def tn(a, b):
    return lax.dot_general(a, b, (((0,), (0,)), ((), ())), preferred_element_type=F32)


def kernel(
    img_hbm, ngain, proj_hbm, kv_hbm, kgain, q_hbm, qgain, hgate, cot_hbm, block_image, image_len,
    out,
    img, proj, kvall, queries, cot,
    wsend, wown, wsib, wys, wyr, wg,
    projf, kvb, qgb, dqbuf, dqo, dqin,
    gsend, gown, gsib, rsb, rxo_in, rx_in, rzo_in, rz_in, ztot,
    pgbuf, acc,
    ssem, rsem, lsem,
):
    g = lax.axis_index("group")
    s = lax.axis_index("seq")
    m = lax.axis_index("mp")
    z, x = s // 4, s % 4
    y, c = m // 2, m % 2
    p = gray(z)
    other = 1 - c

    xs = [x, (x + 1) % 4, (x + 3) % 4, (x + 2) % 4]
    zs = [z, gray((p + 1) % 4), gray((p + 3) % 4), gray((p + 2) % 4)]

    sib = (g, s, 2 * y + other)
    ydev = [None] + [(g, s, 2 * ((y + d) % 4) + c) for d in (1, 2, 3)]
    xdev = [(g, z * 4 + xs[1], m), (g, z * 4 + xs[2], m)]
    zdev = [(g, zs[1] * 4 + x, m), (g, zs[2] * 4 + x, m)]
    across = (1 - g, s, m)
    across_sib = (1 - g, s, 2 * y + other)

    def rc(place, src, dst, dev):
        return pltpu.make_async_remote_copy(
            src_ref=src, dst_ref=dst, send_sem=ssem.at[place], recv_sem=rsem.at[place],
            device_id=dev, device_id_type=MESH,
        )

    def send(place, src, dst, dev):
        copy = rc(place, src, dst, dev)
        copy.start()
        return copy

    def left(place, ref):
        rc(place, ref, ref, sib).wait_send()

    def arrived(place, dst):
        rc(place, dst, dst, sib).wait_recv()

    local = {}

    def load(name, src, dst):
        copy = pltpu.make_async_copy(src, dst, lsem.at[len(local)])
        local[name] = copy
        return copy

    def strip(par, kind, yy):
        return load(
            ("kv", len(local)),
            kv_hbm.at[:, pl.ds(pl.multiple_of((2 * yy + par) * 256 + kind * 128, 128), 128)],
            kvall.at[par, kind, :, yy * 128:(yy + 1) * 128],
        )

    proj_load = load("proj", proj_hbm, proj)
    proj_load.start()
    kv_sib = [strip(g, other, yy) for yy in range(4)]
    for copy in kv_sib:
        copy.start()
    kv_own = [strip(g, c, yy) for yy in range(4)]
    for copy in kv_own:
        copy.start()
    q_load = load("q", q_hbm, queries)
    q_load.start()
    cot_load = load("cot", cot_hbm, cot)
    cot_load.start()
    img_load = load("img", img_hbm, img)
    img_load.start()
    kv_rest = [strip(1 - g, kind, yy) for kind in range(2) for yy in range(4)]

    @pl.when(g == 0)
    def _():
        for copy in kv_rest:
            copy.start()

    barrier = pltpu.get_barrier_semaphore()
    for dev in [sib, *ydev[1:], *xdev, *zdev, across, across_sib]:
        pl.semaphore_signal(barrier, inc=1, device_id=dev, device_id_type=MESH)

    proj_load.wait()
    for copy in kv_sib:
        copy.wait()

    def share_of(r, kind):
        return jnp.dot(
            proj[r * WHALF:(r + 1) * WHALF, :], kvall[g, kind], preferred_element_type=F32
        )

    wsend[0] = share_of(0, other).astype(BF16)
    pl.semaphore_wait(barrier, 10)
    send(BASE["wsib"], wsend.at[0], wsib.at[0], sib)
    wsend[1] = share_of(1, other).astype(BF16)
    send(BASE["wsib"] + 1, wsend.at[1], wsib.at[1], sib)
    for copy in kv_own:
        copy.wait()

    def rows_of(block, r):
        return pl.ds(pl.multiple_of(block * WROWS + r * WHALF, 16), WHALF)

    def wloc(block, r):
        return wg.at[rows_of(block, r), :]

    def kloc(block, r):
        return kvb.at[c, block, r * HALF:(r + 1) * HALF, :]

    def block_of(xrel, zrel):
        return zs[zrel] * 4 + xs[xrel]

    def gather(kind, loc):
        zb, zf = BASE[kind + "z"], BASE[kind + "zf"]
        xb, xf = BASE[kind + "x"], BASE[kind + "xf"]

        def z_own(r):
            ref = loc(block_of(0, 0), r)
            for way in (RIGHT, LEFT):
                send(zb + way * 2 + r, ref, ref, zdev[way])

        def x_direct(zrel, r):
            ref = loc(block_of(0, zrel), r)
            for way in (RIGHT, LEFT):
                send(xb + (way * 4 + zrel) * 2 + r, ref, ref, xdev[way])

        def z_first(way, r):
            zrel = 2 if way == RIGHT else 1
            ref = loc(block_of(0, zrel), r)
            arrived(zb + way * 2 + r, ref)
            if r == way:
                send(zf + way, ref, ref, zdev[way])
            x_direct(zrel, r)

        def z_second(way):
            arrived(zf + way, loc(block_of(0, 3), way))
            x_direct(3, way)

        def x_first(way, zrel, r):
            xrel = 2 if way == RIGHT else 1
            ref = loc(block_of(xrel, zrel), r)
            arrived(xb + (way * 4 + zrel) * 2 + r, ref)
            if r == way:
                send(xf + way * 4 + zrel, ref, ref, xdev[way])

        def x_second(way, zrel):
            arrived(xf + way * 4 + zrel, loc(block_of(3, zrel), way))

        return z_own, x_direct, z_first, z_second, x_first, x_second

    w_z_own, w_x_direct, w_z_first, w_z_second, w_x_first, w_x_second = gather("w", wloc)

    wown[0] = share_of(0, c)
    wown[1] = share_of(1, c)

    def to_y(r):
        arrived(BASE["wsib"] + r, wsib.at[r])
        for yy in range(4):
            cols = slice(yy * 128, (yy + 1) * 128)
            wys[r, yy] = (wown[r, :, cols] + wsib[r, :, cols].astype(F32)).astype(BF16)
        for d in (1, 2, 3):
            send(BASE["wy"] + r * 3 + d - 1, wys.at[r, (y + d) % 4], wyr.at[r, d - 1], ydev[d])

    def own_w(r):
        total = wys[r, y].astype(F32)
        for d in (1, 2, 3):
            arrived(BASE["wy"] + r * 3 + d - 1, wyr.at[r, d - 1])
            total = total + wyr[r, d - 1].astype(F32)
        wg[rows_of(s, r), :] = total.astype(BF16)
        w_z_own(r)
        w_x_direct(0, r)

    to_y(0)
    to_y(1)
    own_w(0)
    own_w(1)

    q_load.wait()
    cot_load.wait()

    @pl.when(c == g)
    def _():
        for h in range(8):
            cols = slice(h * 128, (h + 1) * 128)
            rows = slice((h % 4) * 16, (h % 4 + 1) * 16)
            wide = queries[:, cols].astype(F32)
            scale = lax.rsqrt(jnp.mean(wide * wide, axis=-1, keepdims=True) + epsilon)
            low = (wide * scale * qgain[...]).astype(BF16)
            qgb[h // 4, 0, :, rows, :] = low.reshape(16, 16, HD)
            gate = jnp.tanh(jnp.full((1, HD), hgate[h], F32))
            grad = (cot[:, cols].astype(F32) * gate).astype(BF16)
            qgb[h // 4, 1, :, rows, :] = grad.reshape(16, 16, HD)
        send(BASE["qg"], qgb.at[other], qgb.at[other], sib)

    img_load.wait()
    for part in range(4):
        rows = slice(part * 64, (part + 1) * 64)
        lead = img[rows, :VD].astype(F32)
        center = jnp.mean(lead, axis=-1, keepdims=True)
        spread = jnp.mean((lead - center) ** 2, axis=-1, keepdims=True)
        img[rows, :VD] = ((lead - center) * lax.rsqrt(spread + epsilon) * ngain[...]).astype(BF16)

    for r in (0, 1):
        w_z_first(RIGHT, r)
        w_z_first(LEFT, r)
    for r in (0, 1):
        w_x_first(RIGHT, 0, r)
        w_x_first(LEFT, 0, r)
    w_z_second(RIGHT)
    w_z_second(LEFT)
    for zrel in (1, 2, 3):
        for r in (0, 1):
            w_x_first(RIGHT, zrel, r)
            w_x_first(LEFT, zrel, r)
    for zrel in range(4):
        w_x_second(RIGHT, zrel)
        w_x_second(LEFT, zrel)

    projf[...] = jnp.zeros((ROWS, HD), F32)

    @pl.loop(0, 4)
    def _(part):
        cols = pl.ds(pl.multiple_of(part * 1920, 128), 1920)
        projf[...] += jnp.dot(img[:, cols], wg[cols, :], preferred_element_type=F32)

    made = projf[...]
    key_scale = lax.rsqrt(jnp.mean(made * made, axis=-1, keepdims=True) + epsilon)
    kvb[c, s] = jnp.where(c == 0, made * key_scale * kgain[...], made).astype(BF16)

    k_z_own, k_x_direct, k_z_first, k_z_second, k_x_first, k_x_second = gather("k", kloc)
    k_z_own(0)
    k_z_own(1)
    k_x_direct(0, 0)
    k_x_direct(0, 1)

    def hand_over(it, block):
        send(BASE["share"] + it, kvb.at[c, block], kvb.at[c, block], sib)

    @pl.when(c != g)
    def _():
        arrived(BASE["qg"], qgb.at[c])

    def image_of(it):
        xx = (x + gray(it // 4)) % 4
        zz = gray((p + gray(it % 4)) % 4)
        return zz * 4 + xx

    def finish(it):
        xrel, zrel = it // 4, it % 4
        arrived(BASE["gsib"] + it, gsib.at[it])
        total = gown[it] + gsib[it].astype(F32)
        gown[it] = total
        rsb[it] = total.astype(BF16)

        def go(way, r, base, dst):
            send(base, rsb.at[it, r * HALF:(r + 1) * HALF, :], dst, xdev[way])

        @pl.when(xrel == 1)
        def _():
            go(RIGHT, 1, BASE["rx"] + (RIGHT * 4 + zrel) * 2 + 1, rx_in.at[RIGHT, zrel, 1])

        @pl.when(xrel == 2)
        def _():
            go(LEFT, 0, BASE["rx"] + (LEFT * 4 + zrel) * 2 + 0, rx_in.at[LEFT, zrel, 0])

        @pl.when(xrel == 3)
        def _():
            go(RIGHT, 0, BASE["rxo"] + RIGHT * 4 + zrel, rxo_in.at[RIGHT, zrel])
            go(LEFT, 1, BASE["rxo"] + LEFT * 4 + zrel, rxo_in.at[LEFT, zrel])

    def before(k):
        xrel, zrel = k // 4, k % 4
        if xrel == 0:
            if zrel == 1:
                for r in (0, 1):
                    k_z_first(RIGHT, r)
                    k_z_first(LEFT, r)
            if zrel == 3:
                k_z_second(RIGHT)
                k_z_second(LEFT)
        elif xrel == 1:
            for r in (0, 1):
                k_x_first(LEFT, zrel, r)
                k_x_first(RIGHT, zrel, r)
        elif xrel == 3:
            k_x_second(RIGHT, zrel)
            k_x_second(LEFT, zrel)
        hand_over(k, block_of(xrel, zrel))

    @pl.loop(0, 16)
    def _(it):
        for k in range(16):
            @pl.when(it == k)
            def _(k=k):
                before(k)

        i = image_of(it)
        first, last, seen = i * 0, i * 0, i * 0
        for b in range(16):
            hit = (block_image[b, 0] == i).astype(jnp.int32)
            first = first + b * hit * (1 - seen)
            last = last + (b - last) * hit
            seen = seen + hit * (1 - seen)
        use0 = seen > 0
        use1 = last > first
        at0, at1 = first, last
        zero = jnp.zeros((64, HD), BF16)
        low = jnp.concatenate(
            [jnp.where(use0, qgb[c, 0, at0], zero), jnp.where(use1, qgb[c, 0, at1], zero)], axis=0
        )
        grad = jnp.concatenate(
            [jnp.where(use0, qgb[c, 1, at0], zero), jnp.where(use1, qgb[c, 1, at1], zero)], axis=0
        )
        arrived(BASE["share"] + it, kvb.at[other, i])
        keys, values = kvb[0, i], kvb[1, i]
        scores = nt(keys, low) * INV
        usable = lax.broadcasted_iota(jnp.int32, (ROWS, HD), 0) < image_len[i]
        raised = jnp.where(usable, jnp.exp(scores), 0.0)
        weights = raised / jnp.sum(raised, axis=0, keepdims=True)
        weight_grads = nt(values, grad)
        inner = jnp.sum(weights * weight_grads, axis=0, keepdims=True)
        score_grads = (weights * (weight_grads - inner) * INV).astype(BF16)
        key_grads = jnp.dot(score_grads, low, preferred_element_type=F32)
        value_grads = jnp.dot(weights.astype(BF16), grad, preferred_element_type=F32)
        gown[it] = jnp.where(c == 0, key_grads, value_grads)
        gsend[it] = jnp.where(c == 0, value_grads, key_grads).astype(BF16)
        send(BASE["gsib"] + it, gsend.at[it], gsib.at[it], sib)
        dqbuf[i] = tn(score_grads, keys).astype(BF16).reshape(2, 64, HD)

        @pl.when(it > 0)
        def _():
            finish(it - 1)

    finish(15)

    @pl.loop(0, 16)
    def _(b):
        mine = block_image[b, 0]
        slot = b * 0
        for bb in range(16):
            hit = ((bb < b) & (block_image[bb, 0] == mine)).astype(jnp.int32)
            slot = slot + hit * (1 - slot)
        dqo[b] = dqbuf[mine, slot]

    @pl.when(g == 0)
    def _():
        send(BASE["dq"] + c, dqo, dqin.at[c], (1, s, 2 * y))

    @pl.when((g == 1) & (c == 0))
    def _():
        send(BASE["dq"], dqo, dqin.at[0], sib)

    @pl.when((g == 1) & (c == 1))
    def _():
        dqin[1] = dqo[...]

    def half(r):
        return slice(r * HALF, (r + 1) * HALF)

    for zrel in range(4):
        for way in (RIGHT, LEFT):
            it = (1 if way == RIGHT else 2) * 4 + zrel
            r = way
            arrived(BASE["rxo"] + way * 4 + zrel, rxo_in.at[way, zrel])
            rsb[it, half(r)] = (gown[it, half(r)] + rxo_in[way, zrel].astype(F32)).astype(BF16)
            send(
                BASE["rx"] + (way * 4 + zrel) * 2 + r, rsb.at[it, half(r)], rx_in.at[way, zrel, r],
                xdev[way],
            )

    def x_total(zrel, r):
        total = gown[zrel, half(r)]
        for way in (RIGHT, LEFT):
            arrived(BASE["rx"] + (way * 4 + zrel) * 2 + r, rx_in.at[way, zrel, r])
            total = total + rx_in[way, zrel, r].astype(F32)
        return total

    for r in (0, 1):
        ztot[3, half(r)] = x_total(3, r).astype(BF16)
        send(BASE["rzo"] + r, ztot.at[3, half(r)], rzo_in.at[r], zdev[r])
    for way in (RIGHT, LEFT):
        zrel = 1 if way == RIGHT else 2
        r = 1 - way
        ztot[zrel, half(r)] = x_total(zrel, r).astype(BF16)
        send(BASE["rz"] + way * 2 + r, ztot.at[zrel, half(r)], rz_in.at[way, r], zdev[way])
    for way in (RIGHT, LEFT):
        zrel = 1 if way == RIGHT else 2
        r = way
        total = x_total(zrel, r)
        arrived(BASE["rzo"] + way, rzo_in.at[way])
        ztot[zrel, half(r)] = (total + rzo_in[way].astype(F32)).astype(BF16)
        send(BASE["rz"] + way * 2 + r, ztot.at[zrel, half(r)], rz_in.at[way, r], zdev[way])
    for r in (0, 1):
        total = x_total(0, r)
        for way in (RIGHT, LEFT):
            arrived(BASE["rz"] + way * 2 + r, rz_in.at[way, r])
            total = total + rz_in[way, r].astype(F32)
        raw = projf[half(r)]
        scale = lax.rsqrt(jnp.mean(raw * raw, axis=-1, keepdims=True) + epsilon)
        scaled = total * kgain[...]
        back = scale * (
            scaled - raw * (scale * scale) * jnp.mean(scaled * raw, axis=-1, keepdims=True)
        )
        pgbuf[g, c, y, half(r)] = jnp.where(c == 0, back, total).astype(BF16)

    @pl.when(g == 1)
    def _():
        copy = send(BASE["pgx"], pgbuf.at[1, c, y], pgbuf.at[1, c, y], across)
        for half_of in range(2):
            @pl.when((c == 0) | (half_of == 0))
            def _():
                arrived(BASE["dq"] + half_of, dqin.at[half_of])
        for h in range(8):
            cols = slice(h * 128, (h + 1) * 128)
            rows = slice((h % 4) * 16, (h % 4 + 1) * 16)
            d = dqin[h // 4, :, rows, :].reshape(ROWS, HD).astype(F32) * qgain[...]
            wide = queries[:, cols].astype(F32)
            scale = lax.rsqrt(jnp.mean(wide * wide, axis=-1, keepdims=True) + epsilon)
            res = scale * (d - wide * (scale * scale) * jnp.mean(d * wide, axis=-1, keepdims=True))
            out[0, :, cols] = res.astype(BF16)
        copy.wait_send()

    @pl.when(g == 0)
    def _():
        mine = []
        for par in range(2):
            if par == 1:
                arrived(BASE["pgx"], pgbuf.at[1, c, y])
            for d in (1, 2, 3):
                ref = pgbuf.at[par, c, y]
                mine.append(send(BASE["pgy"] + par * 3 + d - 1, ref, ref, ydev[d]))
            for d in (1, 2, 3):
                arrived(BASE["pgy"] + par * 3 + d - 1, pgbuf.at[par, c, (y + 4 - d) % 4])
            ref = pgbuf.at[par, c]
            mine.append(send(BASE["pgs"] + par, ref, ref, sib))
            if par == 1:
                for copy in kv_rest:
                    copy.wait()

            def term(kind):
                cat = jnp.concatenate([pgbuf[par, kind, yy] for yy in range(4)], axis=1)
                return nt(cat, kvall[par, kind])

            if par == 0:
                acc[...] = term(c)
            else:
                acc[...] += term(c)
            arrived(BASE["pgs"] + par, pgbuf.at[par, other])
            if par == 0:
                acc[...] += term(other)
            else:
                out[0] = (acc[...] + term(other)).astype(BF16)
        for copy in mine:
            copy.wait_send()

    for name, piece in (
        ("wsib", wsend.at[0]),
        ("wy", wys.at[0, 0]),
        ("wz", wg.at[0:WHALF, :]),
        ("wzf", wg.at[0:WHALF, :]),
        ("wx", wg.at[0:WHALF, :]),
        ("wxf", wg.at[0:WHALF, :]),
        ("kz", kvb.at[0, 0, 0:HALF, :]),
        ("kzf", kvb.at[0, 0, 0:HALF, :]),
        ("kx", kvb.at[0, 0, 0:HALF, :]),
        ("kxf", kvb.at[0, 0, 0:HALF, :]),
        ("share", kvb.at[0, 0]),
        ("rx", rsb.at[0, 0:HALF, :]),
        ("rxo", rsb.at[0, 0:HALF, :]),
        ("rzo", ztot.at[0, 0:HALF, :]),
        ("rz", ztot.at[0, 0:HALF, :]),
    ):
        for k in range(_sizes[name]):
            left(BASE[name] + k, piece)

    for it in range(16):
        left(BASE["gsib"] + it, gsend.at[it])
    @pl.when(c == g)
    def _():
        left(BASE["qg"], qgb.at[other])

    @pl.when(g == 0)
    def _():
        left(BASE["dq"] + c, dqo)

    @pl.when((g == 1) & (c == 0))
    def _():
        left(BASE["dq"], dqo)


def per_device(
    image_states, norm_gain, proj_weight, kv_weight, key_gain, queries, query_gain, head_gate,
    cotangent, block_image, image_len,
):
    anywhere = pl.BlockSpec(memory_space=pl.ANY)
    vmem = pl.BlockSpec(memory_space=pltpu.VMEM)
    smem = pl.BlockSpec(memory_space=pltpu.SMEM)
    V = pltpu.VMEM
    scratch = [
        V((ROWS, VIN), BF16),
        V((WROWS, 1024), BF16),
        V((2, 2, 1024, 512), BF16),
        V((ROWS, 1024), BF16),
        V((ROWS, 1024), BF16),
        V((2, WHALF, 512), BF16),
        V((2, WHALF, 512), F32),
        V((2, WHALF, 512), BF16),
        V((2, 4, WHALF, HD), BF16),
        V((2, 3, WHALF, HD), BF16),
        V((VIN, HD), BF16),
        V((ROWS, HD), F32),
        V((2, 16, ROWS, HD), BF16),
        V((2, 2, 16, 64, HD), BF16),
        V((16, 2, 64, HD), BF16),
        V((16, 64, HD), BF16),
        V((2, 16, 64, HD), BF16),
        V((16, ROWS, HD), BF16),
        V((16, ROWS, HD), F32),
        V((16, ROWS, HD), BF16),
        V((16, ROWS, HD), BF16),
        V((2, 4, HALF, HD), BF16),
        V((2, 4, 2, HALF, HD), BF16),
        V((2, HALF, HD), BF16),
        V((2, 2, HALF, HD), BF16),
        V((4, ROWS, HD), BF16),
        V((2, 2, 4, ROWS, HD), BF16),
        V((ROWS, 1024), F32),
        pltpu.SemaphoreType.DMA((PLACES,)),
        pltpu.SemaphoreType.DMA((PLACES,)),
        pltpu.SemaphoreType.DMA((24,)),
    ]
    return pl.pallas_call(
        kernel,
        out_shape=jax.ShapeDtypeStruct((1, ROWS, 1024), BF16),
        in_specs=[
            anywhere, vmem, anywhere, anywhere, vmem, anywhere, vmem, smem, anywhere, smem, smem,
        ],
        out_specs=vmem,
        scratch_shapes=scratch,
        compiler_params=pltpu.CompilerParams(
            collective_id=0, has_side_effects=True, vmem_limit_bytes=48 * 2**20
        ),
    )(
        image_states.reshape(ROWS, VIN), norm_gain.reshape(1, VD), proj_weight, kv_weight,
        key_gain.reshape(1, HD), queries, query_gain.reshape(1, HD), head_gate, cotangent,
        block_image, image_len,
    )


def solution(mesh):
    placed = (
        P("seq", None, None), P(), P("seq", "mp"), P("mp", None), P(), P("seq", "mp"), P(),
        P("mp"), P("seq", "mp"), P("seq", None), P(),
    )
    return jax.shard_map(
        per_device, mesh=mesh, in_specs=placed, out_specs=P("group", "seq", "mp"), check_vma=False
    )
```

```python
import math

import jax
import jax.numpy as jnp
from jax import lax
from jax.experimental import pallas as pl
from jax.experimental.pallas import tpu as pltpu
from jax.sharding import PartitionSpec as P

MESH = pl.DeviceIdType.MESH
F32, BF16 = jnp.float32, jnp.bfloat16
epsilon = 1e-05

VIN, VD, HD = 7680, 1280, 128
ROWS = 256
WROWS = 480
WHALF = WROWS // 2
HALF = ROWS // 2
INV = 1.0 / math.sqrt(HD)

RIGHT, LEFT = 0, 1

_sizes = dict(
    wsib=2, wy=6, route=40,
    wz=6, wx=16, wxf=8,
    share=1, gsib=1,
    pgx=1, pgy=6, pgs=8, back=32,
)
BASE = {}
_total = 0
for _name, _size in _sizes.items():
    BASE[_name] = _total
    _total += _size
PLACES = _total


def gray(k):
    return k + (k // 2) * (1 - 2 * (k % 2))


def nt(a, b):
    return lax.dot_general(a, b, (((1,), (1,)), ((), ())), preferred_element_type=F32)


def tn(a, b):
    return lax.dot_general(a, b, (((0,), (0,)), ((), ())), preferred_element_type=F32)


def kernel(
    img_hbm, ngain_hbm, proj_hbm, kv_hbm, kgain_hbm, q_hbm, qgain_hbm, hgate_hbm, cot_hbm,
    block_image_hbm, image_len_hbm,
    out,
    ngain, kgain, qgain, hgate, block_image, image_len,
    img, proj, kvall, queries, cot,
    wsend, wown, wsib, wys, wyr, wg,
    projf, kvb, qgb, qsend, qin, dqout, dqin, dqs,
    gmade, gsib,
    pgbuf, acc,
    ssem, rsem, lsem,
):
    g = lax.axis_index("group")
    s = lax.axis_index("seq")
    m = lax.axis_index("mp")
    z, x = s // 4, s % 4
    y, c = m // 2, m % 2
    p = gray(z)
    other = 1 - c

    xs = [x, (x + 1) % 4, (x + 3) % 4, (x + 2) % 4]
    zs = [z, gray((p + 1) % 4), gray((p + 3) % 4), gray((p + 2) % 4)]

    sib = (g, s, 2 * y + other)
    ydev = [None] + [(g, s, 2 * ((y + d) % 4) + c) for d in (1, 2, 3)]
    xdev = [(g, z * 4 + xs[1], m), (g, z * 4 + xs[2], m)]
    xfar = (g, z * 4 + xs[3], m)
    zdev = [(g, zs[k] * 4 + x, m) for k in (1, 2, 3)]
    across = (1 - g, s, m)

    def rc(place, src, dst, dev):
        return pltpu.make_async_remote_copy(
            src_ref=src, dst_ref=dst, send_sem=ssem.at[place], recv_sem=rsem.at[place],
            device_id=dev, device_id_type=MESH,
        )

    def send(place, src, dst, dev):
        copy = rc(place, src, dst, dev)
        copy.start()
        return copy

    def left(place, ref):
        rc(place, ref, ref, sib).wait_send()

    def arrived(place, dst):
        rc(place, dst, dst, sib).wait_recv()

    local = {}

    def load(name, src, dst):
        copy = pltpu.make_async_copy(src, dst, lsem.at[len(local)])
        local[name] = copy
        return copy

    def strip(par, kind, yy):
        return load(
            ("kv", len(local)),
            kv_hbm.at[:, pl.ds(pl.multiple_of((2 * yy + par) * 256 + kind * 128, 128), 128)],
            kvall.at[par, kind, :, yy * 128:(yy + 1) * 128],
        )

    proj_load = load("proj", proj_hbm, proj)
    proj_load.start()
    kv_sib = [strip(g, other, yy) for yy in range(4)]
    for copy in kv_sib:
        copy.start()
    kv_own = [strip(g, c, yy) for yy in range(4)]
    for copy in kv_own:
        copy.start()
    q_load = load("q", q_hbm, queries)
    q_load.start()
    cot_load = load("cot", cot_hbm, cot)
    cot_load.start()
    img_load = load("img", img_hbm, img)
    img_load.start()
    small = [
        load("ngain", ngain_hbm, ngain),
        load("kgain", kgain_hbm, kgain),
        load("qgain", qgain_hbm, qgain),
        load("hgate", hgate_hbm, hgate),
        load("block_image", block_image_hbm, block_image),
        load("image_len", image_len_hbm, image_len),
    ]
    for copy in small:
        copy.start()
    kv_rest = [strip(1 - g, kind, yy) for kind in range(2) for yy in range(4)]

    @pl.when(g == 0)
    def _():
        for copy in kv_rest:
            copy.start()

    barrier = pltpu.get_barrier_semaphore()
    for dev in ydev[1:]:
        pl.semaphore_signal(barrier, inc=1, device_id=dev, device_id_type=MESH)

    @pl.loop(1, 64)
    def _(k):
        at = (g * 32 + s * 2 + c + k) % 64
        dev = (at // 32, (at // 2) % 16, 2 * y + at % 2)
        pl.semaphore_signal(barrier, inc=1, device_id=dev, device_id_type=MESH)

    proj_load.wait()
    for copy in kv_sib:
        copy.wait()

    def share_of(r, kind):
        return jnp.dot(
            proj[r * WHALF:(r + 1) * WHALF, :], kvall[g, kind], preferred_element_type=F32
        )

    wsend[0] = share_of(0, other).astype(BF16)
    pl.semaphore_wait(barrier, 66)
    send(BASE["wsib"], wsend.at[0], wsib.at[0], sib)
    wsend[1] = share_of(1, other).astype(BF16)
    send(BASE["wsib"] + 1, wsend.at[1], wsib.at[1], sib)
    for copy in kv_own:
        copy.wait()

    def rows_of(block, r):
        return pl.ds(pl.multiple_of(block * WROWS + r * WHALF, 16), WHALF)

    def wloc(block, r):
        return wg.at[rows_of(block, r), :]

    def block_of(xrel, zrel):
        return zs[zrel] * 4 + xs[xrel]

    def gather(kind, loc):
        zb, xb, xf = BASE[kind + "z"], BASE[kind + "x"], BASE[kind + "xf"]

        def z_own(r):
            ref = loc(block_of(0, 0), r)
            for k in (1, 2, 3):
                send(zb + (k - 1) * 2 + r, ref, ref, zdev[k - 1])

        def x_direct(zrel, r):
            ref = loc(block_of(0, zrel), r)
            for way in (RIGHT, LEFT):
                send(xb + (way * 4 + zrel) * 2 + r, ref, ref, xdev[way])
            if zrel == 3:
                send(xf + r * 4 + zrel, ref, ref, xfar)

        def z_in(zrel, r):
            k = (0, 2, 1, 3)[zrel]
            arrived(zb + (k - 1) * 2 + r, loc(block_of(0, zrel), r))
            x_direct(zrel, r)

        def x_first(way, zrel, r):
            xrel = 2 if way == RIGHT else 1
            ref = loc(block_of(xrel, zrel), r)
            arrived(xb + (way * 4 + zrel) * 2 + r, ref)
            if r == way and zrel != 3:
                send(xf + way * 4 + zrel, ref, ref, xdev[way])

        def x_second(way, zrel):
            arrived(xf + way * 4 + zrel, loc(block_of(3, zrel), way))

        return z_own, x_direct, z_in, x_first, x_second

    w_z_own, w_x_direct, w_z_in, w_x_first, w_x_second = gather("w", wloc)

    wown[0] = share_of(0, c)
    wown[1] = share_of(1, c)

    def to_y(r):
        arrived(BASE["wsib"] + r, wsib.at[r])
        for yy in range(4):
            cols = slice(yy * 128, (yy + 1) * 128)
            wys[r, yy] = (wown[r, :, cols] + wsib[r, :, cols].astype(F32)).astype(BF16)
        for d in (1, 2, 3):
            send(BASE["wy"] + r * 3 + d - 1, wys.at[r, (y + d) % 4], wyr.at[r, d - 1], ydev[d])

    def own_w(r):
        total = wys[r, y].astype(F32)
        for d in (1, 2, 3):
            arrived(BASE["wy"] + r * 3 + d - 1, wyr.at[r, d - 1])
            total = total + wyr[r, d - 1].astype(F32)
        wg[rows_of(s, r), :] = total.astype(BF16)
        w_z_own(r)
        w_x_direct(0, r)

    to_y(0)
    to_y(1)
    for copy in small:
        copy.wait()
    q_load.wait()
    cot_load.wait()
    for h in range(8):
        cols = slice(h * 128, (h + 1) * 128)
        rows = slice((h % 4) * 16, (h % 4 + 1) * 16)
        wide = queries[:, cols].astype(F32)
        scale = lax.rsqrt(jnp.mean(wide * wide, axis=-1, keepdims=True) + epsilon)
        low = (wide * scale * qgain[...]).astype(BF16)
        qgb[h // 4, 0, :, rows, :] = low.reshape(16, 16, HD)
        gate = jnp.tanh(jnp.full((1, HD), hgate[h], F32))
        grad = (cot[:, cols].astype(F32) * gate).astype(BF16)
        qgb[h // 4, 1, :, rows, :] = grad.reshape(16, 16, HD)

    @pl.loop(0, 16)
    def _(i):
        first, last, seen = i * 0, i * 0, i * 0
        for b in range(16):
            hit = (block_image[b] == i).astype(jnp.int32)
            first = first + b * hit * (1 - seen)
            last = last + (b - last) * hit
            seen = seen + hit * (1 - seen)
        zero = jnp.zeros((64, HD), BF16)
        for part in range(2):
            for kind in range(2):
                qsend[i, part, kind, 0] = jnp.where(seen > 0, qgb[part, kind, first], zero)
                qsend[i, part, kind, 1] = jnp.where(last > first, qgb[part, kind, last], zero)

    place_z = g * 4 + z
    for step, dz in enumerate((2, -2, 1, -1, 0)):
        to_z = (place_z + dz + 8) % 8

        @pl.when(to_z // 4 == c)
        def _(step=step, dz=dz, to_z=to_z):
            for xrel in (3, 1, 2, 0):
                owner = (to_z % 4) * 4 + xs[xrel]
                for part in range(2):
                    place = BASE["route"] + (step * 4 + xrel) * 2 + part
                    src, dst = qsend.at[owner, part], qin.at[s]
                    if dz == 2:
                        src, dst = src.at[0], dst.at[0]
                    if dz == -2:
                        src, dst = src.at[1], dst.at[1]
                    if dz == 0 and xrel == 0:
                        @pl.when(c == part)
                        def _(part=part):
                            qin[s] = qsend[s, part]

                        @pl.when(c != part)
                        def _(place=place, src=src, dst=dst):
                            send(place, src, dst, sib)
                    else:
                        send(place, src, dst, (to_z // 4, owner, 2 * y + part))

    own_w(0)
    own_w(1)
    for r in (0, 1):
        w_z_in(1, r)
        w_z_in(2, r)

    img_load.wait()
    for part in range(4):
        rows = slice(part * 64, (part + 1) * 64)
        lead = img[rows, :VD].astype(F32)
        center = jnp.mean(lead, axis=-1, keepdims=True)
        spread = jnp.mean((lead - center) ** 2, axis=-1, keepdims=True)
        lead = (lead - center) * lax.rsqrt(spread + epsilon)
        for k in range(VD // 128):
            cols = slice(k * 128, (k + 1) * 128)
            img[rows, cols] = (lead[:, cols] * ngain[k:k + 1, :]).astype(BF16)

    for r in (0, 1):
        w_x_first(RIGHT, 0, r)
        w_x_first(LEFT, 0, r)
    for r in (0, 1):
        w_z_in(3, r)
    for zrel in (1, 2, 3):
        for r in (0, 1):
            w_x_first(RIGHT, zrel, r)
            w_x_first(LEFT, zrel, r)
    for zrel in range(4):
        w_x_second(RIGHT, zrel)
        w_x_second(LEFT, zrel)
        cols = pl.ds(pl.multiple_of(zs[zrel] * (4 * WROWS), 128), 4 * WROWS)
        product = jnp.dot(img[:, cols], wg[cols, :], preferred_element_type=F32)
        if zrel == 0:
            projf[...] = product
        else:
            projf[...] += product

    made = projf[...]
    key_scale = lax.rsqrt(jnp.mean(made * made, axis=-1, keepdims=True) + epsilon)
    kvb[c] = jnp.where(c == 0, made * key_scale * kgain[...], made).astype(BF16)

    send(BASE["share"], kvb.at[c], kvb.at[c], sib)

    for step, dz in enumerate((2, -2, 1, -1, 0)):
        from_z = (z + 8 - dz) % 4
        for xrel in range(4):
            text = from_z * 4 + (x + (0, 3, 1, 2)[xrel]) % 4
            place = BASE["route"] + (step * 4 + xrel) * 2 + c
            dst = qin.at[text]
            if dz == 2:
                dst = dst.at[0]
            if dz == -2:
                dst = dst.at[1]
            if dz == 0 and xrel == 0:
                @pl.when(c != g)
                def _(place=place, dst=dst):
                    arrived(place, dst)
            else:
                arrived(place, dst)
    arrived(BASE["share"], kvb.at[other])

    gmade[...] = jnp.zeros((2, ROWS, HD), F32)

    @pl.loop(0, 8)
    def _(step):
        zz = (z + step // 2) % 4
        devices = [zz * 4 + (step % 2) * 2 + k for k in range(2)]
        low = jnp.concatenate([qin[t, 0].reshape(128, HD) for t in devices], axis=0)
        grad = jnp.concatenate([qin[t, 1].reshape(128, HD) for t in devices], axis=0)
        keys, values = kvb[0], kvb[1]
        scores = nt(keys, low) * INV
        usable = lax.broadcasted_iota(jnp.int32, (ROWS, ROWS), 0) < image_len[s]
        raised = jnp.where(usable, jnp.exp(scores), 0.0)
        weights = raised / jnp.sum(raised, axis=0, keepdims=True)
        weight_grads = nt(values, grad)
        inner = jnp.sum(weights * weight_grads, axis=0, keepdims=True)
        score_grads = (weights * (weight_grads - inner) * INV).astype(BF16)
        gmade[0] += jnp.dot(score_grads, low, preferred_element_type=F32)
        gmade[1] += jnp.dot(weights.astype(BF16), grad, preferred_element_type=F32)
        back = tn(score_grads, keys).astype(BF16)
        for k, t in enumerate(devices):
            dqout[t] = back[k * 128:(k + 1) * 128].reshape(2, 64, HD)

            place = BASE["back"] + ((16 + t - s) % 16) * 2 + c
            here = (g == 1) & (c == 1) & (t == s)

            @pl.when(here)
            def _(t=t):
                dqin[s, 1] = dqout[t]

            @pl.when(jnp.logical_not(here))
            def _(t=t, place=place):
                send(place, dqout.at[t], dqin.at[s, c], (1, t, 2 * y + g))

    send(BASE["gsib"], gmade.at[other], gsib, sib)
    arrived(BASE["gsib"], gsib)

    def half(r):
        return slice(r * HALF, (r + 1) * HALF)

    for r in (0, 1):
        total = gmade[c, half(r)] + gsib[half(r)]
        raw = projf[half(r)]
        scale = lax.rsqrt(jnp.mean(raw * raw, axis=-1, keepdims=True) + epsilon)
        scaled = total * kgain[...]
        back = scale * (
            scaled - raw * (scale * scale) * jnp.mean(scaled * raw, axis=-1, keepdims=True)
        )
        pgbuf[g, c, y, half(r)] = jnp.where(c == 0, back, total).astype(BF16)

    @pl.when(g == 1)
    def _():
        copy = send(BASE["pgx"], pgbuf.at[1, c, y], pgbuf.at[1, c, y], across)
        for image in range(16):
            for part in range(2):
                place = BASE["back"] + ((16 + s - image) % 16) * 2 + part
                if part == 0:
                    arrived(place, dqin.at[image, part])
                else:
                    @pl.when((c == 0) | (s != image))
                    def _(place=place, image=image):
                        arrived(place, dqin.at[image, 1])

        @pl.loop(0, 16)
        def _(b):
            mine = block_image[b]
            slot = b * 0
            for bb in range(16):
                hit = ((bb < b) & (block_image[bb] == mine)).astype(jnp.int32)
                slot = slot + hit * (1 - slot)
            for part in range(2):
                dqs[part, b] = dqin[mine, part, slot]

        for h in range(8):
            cols = slice(h * 128, (h + 1) * 128)
            rows = slice((h % 4) * 16, (h % 4 + 1) * 16)
            d = dqs[h // 4, :, rows, :].reshape(ROWS, HD).astype(F32) * qgain[...]
            wide = queries[:, cols].astype(F32)
            scale = lax.rsqrt(jnp.mean(wide * wide, axis=-1, keepdims=True) + epsilon)
            res = scale * (d - wide * (scale * scale) * jnp.mean(d * wide, axis=-1, keepdims=True))
            out[0, :, cols] = res.astype(BF16)
        copy.wait_send()

    @pl.when(g == 0)
    def _():
        mine = []
        for par in range(2):
            if par == 1:
                arrived(BASE["pgx"], pgbuf.at[1, c, y])
            own = pgbuf.at[par, c, y]
            for d in (2, 1, 3):
                mine.append(send(BASE["pgy"] + par * 3 + d - 1, own, own, ydev[d]))
            mine.append(send(BASE["pgs"] + par * 4, own, own, sib))
            for d in (1, 3, 2):
                ref = pgbuf.at[par, c, (y + 4 - d) % 4]
                arrived(BASE["pgy"] + par * 3 + d - 1, ref)
                mine.append(send(BASE["pgs"] + par * 4 + d, ref, ref, sib))
            if par == 1:
                for copy in kv_rest:
                    copy.wait()

            def term(kind):
                cat = jnp.concatenate([pgbuf[par, kind, yy] for yy in range(4)], axis=1)
                return nt(cat, kvall[par, kind])

            if par == 0:
                acc[...] = term(c)
            else:
                acc[...] += term(c)
            for d in (0, 1, 3, 2):
                arrived(BASE["pgs"] + par * 4 + d, pgbuf.at[par, other, (y + 4 - d) % 4])
            if par == 0:
                acc[...] += term(other)
            else:
                out[0] = (acc[...] + term(other)).astype(BF16)
        for copy in mine:
            copy.wait_send()

    for name, piece in (
        ("wsib", wsend.at[0]),
        ("wy", wys.at[0, 0]),
        ("wz", wg.at[0:WHALF, :]),
        ("wx", wg.at[0:WHALF, :]),
        ("wxf", wg.at[0:WHALF, :]),
        ("share", kvb.at[0]),
        ("gsib", gsib),
    ):
        for k in range(_sizes[name]):
            left(BASE[name] + k, piece)

    for step, dz in enumerate((2, -2, 1, -1, 0)):
        to_z = (place_z + dz + 8) % 8

        @pl.when(to_z // 4 == c)
        def _(step=step, dz=dz):
            piece = qsend.at[0, 0, 0] if abs(dz) == 2 else qsend.at[0, 0]
            for xrel in range(4):
                for part in range(2):
                    place = BASE["route"] + (step * 4 + xrel) * 2 + part
                    if dz == 0 and xrel == 0:
                        @pl.when(c != part)
                        def _(place=place):
                            left(place, piece)
                    else:
                        left(place, piece)

    for far in range(16):
        if far == 0:
            @pl.when((g == 0) | (c == 0))
            def _():
                left(BASE["back"] + c, dqout.at[0])
        else:
            left(BASE["back"] + far * 2 + c, dqout.at[0])


def per_device(
    image_states, norm_gain, proj_weight, kv_weight, key_gain, queries, query_gain, head_gate,
    cotangent, block_image, image_len,
):
    anywhere = pl.BlockSpec(memory_space=pl.ANY)
    vmem = pl.BlockSpec(memory_space=pltpu.VMEM)
    V = pltpu.VMEM
    scratch = [
        V((VD // 128, 128), F32),
        V((1, HD), F32),
        V((1, HD), F32),
        pltpu.SMEM((8,), F32),
        pltpu.SMEM((16,), jnp.int32),
        pltpu.SMEM((16,), jnp.int32),
        V((ROWS, VIN), BF16),
        V((WROWS, 1024), BF16),
        V((2, 2, 1024, 512), BF16),
        V((ROWS, 1024), BF16),
        V((ROWS, 1024), BF16),
        V((2, WHALF, 512), BF16),
        V((2, WHALF, 512), F32),
        V((2, WHALF, 512), BF16),
        V((2, 4, WHALF, HD), BF16),
        V((2, 3, WHALF, HD), BF16),
        V((VIN, HD), BF16),
        V((ROWS, HD), F32),
        V((2, ROWS, HD), BF16),
        V((2, 2, 16, 64, HD), BF16),
        V((16, 2, 2, 2, 64, HD), BF16),
        V((16, 2, 2, 64, HD), BF16),
        V((16, 2, 64, HD), BF16),
        V((16, 2, 2, 64, HD), BF16),
        V((2, 16, 64, HD), BF16),
        V((2, ROWS, HD), F32),
        V((ROWS, HD), F32),
        V((2, 2, 4, ROWS, HD), BF16),
        V((ROWS, 1024), F32),
        pltpu.SemaphoreType.DMA((PLACES,)),
        pltpu.SemaphoreType.DMA((PLACES,)),
        pltpu.SemaphoreType.DMA((32,)),
    ]
    return pl.pallas_call(
        kernel,
        out_shape=jax.ShapeDtypeStruct((1, ROWS, 1024), BF16),
        in_specs=[anywhere] * 11,
        out_specs=vmem,
        scratch_shapes=scratch,
        compiler_params=pltpu.CompilerParams(
            collective_id=0, has_side_effects=True, vmem_limit_bytes=60 * 2**20
        ),
    )(
        image_states.reshape(ROWS, VIN), norm_gain.reshape(VD // 128, 128), proj_weight, kv_weight,
        key_gain.reshape(1, HD), queries, query_gain.reshape(1, HD), head_gate, cotangent,
        block_image.reshape(16), image_len,
    )


def solution(mesh):
    placed = (
        P("seq", None, None), P(), P("seq", "mp"), P("mp", None), P(), P("seq", "mp"), P(),
        P("mp"), P("seq", "mp"), P("seq", None), P(),
    )
    return jax.shard_map(
        per_device, mesh=mesh, in_specs=placed, out_specs=P("group", "seq", "mp"), check_vma=False
    )
```

```python
import math

import jax
import jax.numpy as jnp
from jax import lax
from jax.experimental import pallas as pl
from jax.experimental.pallas import tpu as pltpu
from jax.sharding import PartitionSpec as P

MESH = pl.DeviceIdType.MESH
F32, BF16 = jnp.float32, jnp.bfloat16
epsilon = 1e-05

VIN, VD, HD = 7680, 1280, 128
ROWS = 256
WROWS = 480
WHALF = WROWS // 2
HALF = ROWS // 2
INV = 1.0 / math.sqrt(HD)

RIGHT, LEFT = 0, 1

_sizes = dict(
    wsib=2, wy=6, route=40,
    wz=6, wx=16, wxf=8,
    share=1, gsib=1,
    pgx=1, pgy=6, pgs=8, back=32,
)
BASE = {}
_total = 0
for _name, _size in _sizes.items():
    BASE[_name] = _total
    _total += _size
PLACES = _total


def gray(k):
    return k + (k // 2) * (1 - 2 * (k % 2))


def nt(a, b):
    return lax.dot_general(a, b, (((1,), (1,)), ((), ())), preferred_element_type=F32)


def tn(a, b):
    return lax.dot_general(a, b, (((0,), (0,)), ((), ())), preferred_element_type=F32)


def kernel(
    img_hbm, ngain_hbm, proj_hbm, kv_hbm, kgain_hbm, q_hbm, qgain_hbm, hgate_hbm, cot_hbm,
    block_image_hbm, image_len_hbm,
    out,
    ngain, kgain, qgain, hgate, block_image, image_len,
    img, proj, kvall, queries, cot,
    wsend, wown, wsib, wys, wyr, wg,
    projf, kvb, qsend, qin, dqout, dqin, dqs,
    gmade, gsib,
    pgbuf, acc,
    ssem, rsem, lsem,
):
    g = lax.axis_index("group")
    s = lax.axis_index("seq")
    m = lax.axis_index("mp")
    z, x = s // 4, s % 4
    y, c = m // 2, m % 2
    p = gray(z)
    other = 1 - c

    xs = [x, (x + 1) % 4, (x + 3) % 4, (x + 2) % 4]
    zs = [z, gray((p + 1) % 4), gray((p + 3) % 4), gray((p + 2) % 4)]

    sib = (g, s, 2 * y + other)
    ydev = [None] + [(g, s, 2 * ((y + d) % 4) + c) for d in (1, 2, 3)]
    xdev = [(g, z * 4 + xs[1], m), (g, z * 4 + xs[2], m)]
    xfar = (g, z * 4 + xs[3], m)
    zdev = [(g, zs[k] * 4 + x, m) for k in (1, 2, 3)]
    across = (1 - g, s, m)

    def rc(place, src, dst, dev):
        return pltpu.make_async_remote_copy(
            src_ref=src, dst_ref=dst, send_sem=ssem.at[place], recv_sem=rsem.at[place],
            device_id=dev, device_id_type=MESH,
        )

    def send(place, src, dst, dev):
        copy = rc(place, src, dst, dev)
        copy.start()
        return copy

    def left(place, ref):
        rc(place, ref, ref, sib).wait_send()

    def arrived(place, dst):
        rc(place, dst, dst, sib).wait_recv()

    barrier = pltpu.get_barrier_semaphore()
    for dev in ydev[1:]:
        pl.semaphore_signal(barrier, inc=1, device_id=dev, device_id_type=MESH)

    @pl.loop(1, 64)
    def _(k):
        at = (g * 32 + s * 2 + c + k) % 64
        dev = (at // 32, (at // 2) % 16, 2 * y + at % 2)
        pl.semaphore_signal(barrier, inc=1, device_id=dev, device_id_type=MESH)

    local = {}

    def load(name, src, dst):
        copy = pltpu.make_async_copy(src, dst, lsem.at[len(local)])
        local[name] = copy
        return copy

    def strip(par, kind, yy):
        return load(
            ("kv", len(local)),
            kv_hbm.at[:, pl.ds(pl.multiple_of((2 * yy + par) * 256 + kind * 128, 128), 128)],
            kvall.at[par, kind, :, yy * 128:(yy + 1) * 128],
        )

    small = [
        load("ngain", ngain_hbm, ngain),
        load("kgain", kgain_hbm, kgain),
        load("qgain", qgain_hbm, qgain),
        load("hgate", hgate_hbm, hgate),
        load("block_image", block_image_hbm, block_image),
        load("image_len", image_len_hbm, image_len),
    ]
    for copy in small:
        copy.start()
    q_load = load("q", q_hbm, queries)
    q_load.start()
    cot_load = load("cot", cot_hbm, cot)
    cot_load.start()
    proj_load = load("proj", proj_hbm, proj)
    proj_load.start()
    kv_sib = [strip(g, other, yy) for yy in range(4)]
    for copy in kv_sib:
        copy.start()
    kv_own = [strip(g, c, yy) for yy in range(4)]
    for copy in kv_own:
        copy.start()
    img_load = load("img", img_hbm, img)
    img_load.start()
    kv_rest = [strip(1 - g, kind, yy) for kind in range(2) for yy in range(4)]

    @pl.when(g == 0)
    def _():
        for copy in kv_rest:
            copy.start()

    for copy in small:
        copy.wait()
    q_load.wait()
    cot_load.wait()
    gates = [jnp.tanh(jnp.full((1, HD), hgate[h], F32)) for h in range(8)]

    @pl.loop(0, 16)
    def _(i):
        first, last, seen = i * 0, i * 0, i * 0
        for b in range(16):
            hit = (block_image[b] == i).astype(jnp.int32)
            first = first + b * hit * (1 - seen)
            last = last + (b - last) * hit
            seen = seen + hit * (1 - seen)
        zero = jnp.zeros((16, HD), BF16)
        for slot, (at, use) in enumerate(((first, seen > 0), (last, last > first))):
            for h in range(8):
                cols = slice(h * 128, (h + 1) * 128)
                rows = slice((h % 4) * 16, (h % 4 + 1) * 16)
                qsend[i, h // 4, 0, slot, rows, :] = jnp.where(use, queries[at, :, cols], zero)
                grad = (cot[at, :, cols].astype(F32) * gates[h]).astype(BF16)
                qsend[i, h // 4, 1, slot, rows, :] = jnp.where(use, grad, zero)

    pl.semaphore_wait(barrier, 66)

    place_z = g * 4 + z
    for step, dz in enumerate((2, -2, 1, -1, 0)):
        to_z = (place_z + dz + 8) % 8

        @pl.when(to_z // 4 == c)
        def _(step=step, dz=dz, to_z=to_z):
            for xrel in (3, 1, 2, 0):
                owner = (to_z % 4) * 4 + xs[xrel]
                for part in range(2):
                    place = BASE["route"] + (step * 4 + xrel) * 2 + part
                    src, dst = qsend.at[owner, part], qin.at[s]
                    if dz == 2:
                        src, dst = src.at[0], dst.at[0]
                    if dz == -2:
                        src, dst = src.at[1], dst.at[1]
                    if dz == 0 and xrel == 0:
                        @pl.when(c == part)
                        def _(part=part):
                            qin[s] = qsend[s, part]

                        @pl.when(c != part)
                        def _(place=place, src=src, dst=dst):
                            send(place, src, dst, sib)
                    else:
                        send(place, src, dst, (to_z // 4, owner, 2 * y + part))

    proj_load.wait()
    for copy in kv_sib:
        copy.wait()

    def share_of(r, kind):
        return jnp.dot(
            proj[r * WHALF:(r + 1) * WHALF, :], kvall[g, kind], preferred_element_type=F32
        )

    wsend[0] = share_of(0, other).astype(BF16)
    send(BASE["wsib"], wsend.at[0], wsib.at[0], sib)
    wsend[1] = share_of(1, other).astype(BF16)
    send(BASE["wsib"] + 1, wsend.at[1], wsib.at[1], sib)
    for copy in kv_own:
        copy.wait()

    def rows_of(block, r):
        return pl.ds(pl.multiple_of(block * WROWS + r * WHALF, 16), WHALF)

    def wloc(block, r):
        return wg.at[rows_of(block, r), :]

    def block_of(xrel, zrel):
        return zs[zrel] * 4 + xs[xrel]

    def gather(kind, loc):
        zb, xb, xf = BASE[kind + "z"], BASE[kind + "x"], BASE[kind + "xf"]

        def z_own(r):
            ref = loc(block_of(0, 0), r)
            for k in (1, 2, 3):
                send(zb + (k - 1) * 2 + r, ref, ref, zdev[k - 1])

        def x_direct(zrel, r):
            ref = loc(block_of(0, zrel), r)
            for way in (RIGHT, LEFT):
                send(xb + (way * 4 + zrel) * 2 + r, ref, ref, xdev[way])
            if zrel == 3:
                send(xf + r * 4 + zrel, ref, ref, xfar)

        def z_in(zrel, r):
            k = (0, 2, 1, 3)[zrel]
            arrived(zb + (k - 1) * 2 + r, loc(block_of(0, zrel), r))
            x_direct(zrel, r)

        def x_first(way, zrel, r):
            xrel = 2 if way == RIGHT else 1
            ref = loc(block_of(xrel, zrel), r)
            arrived(xb + (way * 4 + zrel) * 2 + r, ref)
            if r == way and zrel != 3:
                send(xf + way * 4 + zrel, ref, ref, xdev[way])

        def x_second(way, zrel):
            arrived(xf + way * 4 + zrel, loc(block_of(3, zrel), way))

        return z_own, x_direct, z_in, x_first, x_second

    w_z_own, w_x_direct, w_z_in, w_x_first, w_x_second = gather("w", wloc)

    wown[0] = share_of(0, c)
    wown[1] = share_of(1, c)

    def to_y(r):
        arrived(BASE["wsib"] + r, wsib.at[r])
        for yy in range(4):
            cols = slice(yy * 128, (yy + 1) * 128)
            wys[r, yy] = (wown[r, :, cols] + wsib[r, :, cols].astype(F32)).astype(BF16)
        for d in (1, 2, 3):
            send(BASE["wy"] + r * 3 + d - 1, wys.at[r, (y + d) % 4], wyr.at[r, d - 1], ydev[d])

    def own_w(r):
        total = wys[r, y].astype(F32)
        for d in (1, 2, 3):
            arrived(BASE["wy"] + r * 3 + d - 1, wyr.at[r, d - 1])
            total = total + wyr[r, d - 1].astype(F32)
        wg[rows_of(s, r), :] = total.astype(BF16)
        w_z_own(r)
        w_x_direct(0, r)

    to_y(0)
    to_y(1)
    own_w(0)
    own_w(1)
    for r in (0, 1):
        w_z_in(1, r)
        w_z_in(2, r)

    def route_in(step, dz):
        from_z = (z + 8 - dz) % 4
        for xrel in range(4):
            text = from_z * 4 + (x + (0, 3, 1, 2)[xrel]) % 4
            place = BASE["route"] + (step * 4 + xrel) * 2 + c
            dst = qin.at[text]
            if dz == 2:
                dst = dst.at[0]
            if dz == -2:
                dst = dst.at[1]
            if dz == 0 and xrel == 0:
                @pl.when(c != g)
                def _(place=place, dst=dst):
                    arrived(place, dst)
            else:
                arrived(place, dst)
            if dz != -2:
                wide = qin[text, 0].reshape(128, HD).astype(F32)
                scale = lax.rsqrt(jnp.mean(wide * wide, axis=-1, keepdims=True) + epsilon)
                qin[text, 0] = (wide * scale * qgain[...]).astype(BF16).reshape(2, 64, HD)

    img_load.wait()
    for part in range(4):
        rows = slice(part * 64, (part + 1) * 64)
        lead = img[rows, :VD].astype(F32)
        center = jnp.mean(lead, axis=-1, keepdims=True)
        spread = jnp.mean((lead - center) ** 2, axis=-1, keepdims=True)
        lead = (lead - center) * lax.rsqrt(spread + epsilon)
        for k in range(VD // 128):
            cols = slice(k * 128, (k + 1) * 128)
            img[rows, cols] = (lead[:, cols] * ngain[k:k + 1, :]).astype(BF16)

    for r in (0, 1):
        w_x_first(RIGHT, 0, r)
        w_x_first(LEFT, 0, r)
    for r in (0, 1):
        w_z_in(3, r)
    route_in(0, 2)
    route_in(1, -2)
    for zrel in (1, 2, 3):
        for r in (0, 1):
            w_x_first(RIGHT, zrel, r)
            w_x_first(LEFT, zrel, r)
        route_in(zrel + 1, (1, -1, 0)[zrel - 1])
    for zrel in range(4):
        w_x_second(RIGHT, zrel)
        w_x_second(LEFT, zrel)
        cols = pl.ds(pl.multiple_of(zs[zrel] * (4 * WROWS), 128), 4 * WROWS)
        product = jnp.dot(img[:, cols], wg[cols, :], preferred_element_type=F32)
        if zrel == 0:
            projf[...] = product
        else:
            projf[...] += product

    made = projf[...]
    key_scale = lax.rsqrt(jnp.mean(made * made, axis=-1, keepdims=True) + epsilon)
    kvb[c] = jnp.where(c == 0, made * key_scale * kgain[...], made).astype(BF16)

    send(BASE["share"], kvb.at[c], kvb.at[c], sib)

    arrived(BASE["share"], kvb.at[other])

    def give_back(t):
        here = (g == 1) & (c == 1) & (t == s)

        @pl.when(here)
        def _():
            dqin[s, 1] = dqout[t]

        @pl.when(jnp.logical_not(here))
        def _():
            place = BASE["back"] + ((16 + t - s) % 16) * 2 + c
            send(place, dqout.at[t], dqin.at[s, c], (1, t, 2 * y + g))

    gmade[...] = jnp.zeros((2, ROWS, HD), F32)

    @pl.loop(0, 8, unroll=2)
    def _(step):
        zz = (z + step // 2) % 4
        devices = [zz * 4 + (step % 2) * 2 + k for k in range(2)]
        low = jnp.concatenate([qin[t, 0].reshape(128, HD) for t in devices], axis=0)
        grad = jnp.concatenate([qin[t, 1].reshape(128, HD) for t in devices], axis=0)
        keys, values = kvb[0], kvb[1]
        scores = nt(keys, low) * INV
        usable = lax.broadcasted_iota(jnp.int32, (ROWS, ROWS), 0) < image_len[s]
        raised = jnp.where(usable, jnp.exp(scores), 0.0)
        over = 1.0 / jnp.sum(raised, axis=0, keepdims=True)
        weight_grads = nt(values, grad)
        inner = jnp.sum(raised * weight_grads, axis=0, keepdims=True) * over
        score_grads = (raised * (over * INV) * (weight_grads - inner)).astype(BF16)
        gmade[0] += jnp.dot(score_grads, low, preferred_element_type=F32)
        gmade[1] += jnp.dot((raised * over).astype(BF16), grad, preferred_element_type=F32)
        back = tn(score_grads, keys).astype(BF16)
        for k, t in enumerate(devices):
            dqout[t] = back[k * 128:(k + 1) * 128].reshape(2, 64, HD)


            @pl.when(g == 0)
            def _(t=t):
                give_back(t)

    send(BASE["gsib"], gmade.at[other], gsib, sib)

    arrived(BASE["gsib"], gsib)

    def half(r):
        return slice(r * HALF, (r + 1) * HALF)

    for r in (0, 1):
        total = gmade[c, half(r)] + gsib[half(r)]
        raw = projf[half(r)]
        scale = lax.rsqrt(jnp.mean(raw * raw, axis=-1, keepdims=True) + epsilon)
        scaled = total * kgain[...]
        back = scale * (
            scaled - raw * (scale * scale) * jnp.mean(scaled * raw, axis=-1, keepdims=True)
        )
        pgbuf[g, c, y, half(r)] = jnp.where(c == 0, back, total).astype(BF16)

    @pl.when(g == 1)
    def _():
        copy = send(BASE["pgx"], pgbuf.at[1, c, y], pgbuf.at[1, c, y], across)

        @pl.loop(0, 16)
        def _(far):
            give_back((s + far) % 16)

        for image in range(16):
            for part in range(2):
                place = BASE["back"] + ((16 + s - image) % 16) * 2 + part
                if part == 0:
                    arrived(place, dqin.at[image, part])
                else:
                    @pl.when((c == 0) | (s != image))
                    def _(place=place, image=image):
                        arrived(place, dqin.at[image, 1])

        @pl.loop(0, 16)
        def _(b):
            mine = block_image[b]
            slot = b * 0
            for bb in range(16):
                hit = ((bb < b) & (block_image[bb] == mine)).astype(jnp.int32)
                slot = slot + hit * (1 - slot)
            for part in range(2):
                dqs[part, b] = dqin[mine, part, slot]

        for h in range(8):
            cols = slice(h * 128, (h + 1) * 128)
            rows = slice((h % 4) * 16, (h % 4 + 1) * 16)
            d = dqs[h // 4, :, rows, :].reshape(ROWS, HD).astype(F32) * qgain[...]
            wide = queries[:, :, cols].reshape(ROWS, HD).astype(F32)
            scale = lax.rsqrt(jnp.mean(wide * wide, axis=-1, keepdims=True) + epsilon)
            res = scale * (d - wide * (scale * scale) * jnp.mean(d * wide, axis=-1, keepdims=True))
            out[0, :, cols] = res.astype(BF16)
        copy.wait_send()

    @pl.when(g == 0)
    def _():
        mine = []
        for par in range(2):
            if par == 1:
                arrived(BASE["pgx"], pgbuf.at[1, c, y])
            own = pgbuf.at[par, c, y]
            for d in (2, 1, 3):
                mine.append(send(BASE["pgy"] + par * 3 + d - 1, own, own, ydev[d]))
            mine.append(send(BASE["pgs"] + par * 4, own, own, sib))
            for d in (1, 3, 2):
                ref = pgbuf.at[par, c, (y + 4 - d) % 4]
                arrived(BASE["pgy"] + par * 3 + d - 1, ref)
                mine.append(send(BASE["pgs"] + par * 4 + d, ref, ref, sib))
            if par == 1:
                for copy in kv_rest:
                    copy.wait()

            def term(kind):
                cat = jnp.concatenate([pgbuf[par, kind, yy] for yy in range(4)], axis=1)
                return nt(cat, kvall[par, kind])

            if par == 0:
                acc[...] = term(c)
            else:
                acc[...] += term(c)
            for d in (0, 1, 3, 2):
                arrived(BASE["pgs"] + par * 4 + d, pgbuf.at[par, other, (y + 4 - d) % 4])
            if par == 0:
                acc[...] += term(other)
            else:
                out[0] = (acc[...] + term(other)).astype(BF16)
        for copy in mine:
            copy.wait_send()

    for name, piece in (
        ("wsib", wsend.at[0]),
        ("wy", wys.at[0, 0]),
        ("wz", wg.at[0:WHALF, :]),
        ("wx", wg.at[0:WHALF, :]),
        ("wxf", wg.at[0:WHALF, :]),
        ("share", kvb.at[0]),
        ("gsib", gsib),
    ):
        for k in range(_sizes[name]):
            left(BASE[name] + k, piece)

    for step, dz in enumerate((2, -2, 1, -1, 0)):
        to_z = (place_z + dz + 8) % 8

        @pl.when(to_z // 4 == c)
        def _(step=step, dz=dz):
            piece = qsend.at[0, 0, 0] if abs(dz) == 2 else qsend.at[0, 0]
            for xrel in range(4):
                for part in range(2):
                    place = BASE["route"] + (step * 4 + xrel) * 2 + part
                    if dz == 0 and xrel == 0:
                        @pl.when(c != part)
                        def _(place=place):
                            left(place, piece)
                    else:
                        left(place, piece)

    for far in range(16):
        if far == 0:
            @pl.when((g == 0) | (c == 0))
            def _():
                left(BASE["back"] + c, dqout.at[0])
        else:
            left(BASE["back"] + far * 2 + c, dqout.at[0])


def per_device(
    image_states, norm_gain, proj_weight, kv_weight, key_gain, queries, query_gain, head_gate,
    cotangent, block_image, image_len,
):
    anywhere = pl.BlockSpec(memory_space=pl.ANY)
    vmem = pl.BlockSpec(memory_space=pltpu.VMEM)
    V = pltpu.VMEM
    scratch = [
        V((VD // 128, 128), F32),
        V((1, HD), F32),
        V((1, HD), F32),
        pltpu.SMEM((8,), F32),
        pltpu.SMEM((16,), jnp.int32),
        pltpu.SMEM((16,), jnp.int32),
        V((ROWS, VIN), BF16),
        V((WROWS, 1024), BF16),
        V((2, 2, 1024, 512), BF16),
        V((16, 16, 1024), BF16),
        V((16, 16, 1024), BF16),
        V((2, WHALF, 512), BF16),
        V((2, WHALF, 512), F32),
        V((2, WHALF, 512), BF16),
        V((2, 4, WHALF, HD), BF16),
        V((2, 3, WHALF, HD), BF16),
        V((VIN, HD), BF16),
        V((ROWS, HD), F32),
        V((2, ROWS, HD), BF16),
        V((16, 2, 2, 2, 64, HD), BF16),
        V((16, 2, 2, 64, HD), BF16),
        V((16, 2, 64, HD), BF16),
        V((16, 2, 2, 64, HD), BF16),
        V((2, 16, 64, HD), BF16),
        V((2, ROWS, HD), F32),
        V((ROWS, HD), F32),
        V((2, 2, 4, ROWS, HD), BF16),
        V((ROWS, 1024), F32),
        pltpu.SemaphoreType.DMA((PLACES,)),
        pltpu.SemaphoreType.DMA((PLACES,)),
        pltpu.SemaphoreType.DMA((32,)),
    ]
    return pl.pallas_call(
        kernel,
        out_shape=jax.ShapeDtypeStruct((1, ROWS, 1024), BF16),
        in_specs=[anywhere] * 11,
        out_specs=vmem,
        scratch_shapes=scratch,
        compiler_params=pltpu.CompilerParams(
            collective_id=0, has_side_effects=True, vmem_limit_bytes=60 * 2**20
        ),
    )(
        image_states.reshape(ROWS, VIN), norm_gain.reshape(VD // 128, 128), proj_weight, kv_weight,
        key_gain.reshape(1, HD), queries.reshape(16, 16, 1024), query_gain.reshape(1, HD),
        head_gate, cotangent.reshape(16, 16, 1024),
        block_image.reshape(16), image_len,
    )


def solution(mesh):
    placed = (
        P("seq", None, None), P(), P("seq", "mp"), P("mp", None), P(), P("seq", "mp"), P(),
        P("mp"), P("seq", "mp"), P("seq", None), P(),
    )
    return jax.shard_map(
        per_device, mesh=mesh, in_specs=placed, out_specs=P("group", "seq", "mp"), check_vma=False
    )
```

```python
import math

import jax
import jax.numpy as jnp
from jax import lax
from jax.experimental import pallas as pl
from jax.experimental.pallas import tpu as pltpu
from jax.sharding import PartitionSpec as P

MESH = pl.DeviceIdType.MESH
F32, BF16 = jnp.float32, jnp.bfloat16
epsilon = 1e-05

VIN, VD, HD = 7680, 1280, 128
ROWS = 256
WROWS = 480
WHALF = WROWS // 2
HALF = ROWS // 2
INV = 1.0 / math.sqrt(HD)

RIGHT, LEFT = 0, 1

_sizes = dict(
    wsib=4, wy=12, route=40,
    wz=6, wx=16, wxf=8,
    share=1, gsib=1,
    pgx=1, pgy=6, pgs=8, back=32,
)
BASE = {}
_total = 0
for _name, _size in _sizes.items():
    BASE[_name] = _total
    _total += _size
PLACES = _total


def gray(k):
    return k + (k // 2) * (1 - 2 * (k % 2))


def nt(a, b):
    return lax.dot_general(a, b, (((1,), (1,)), ((), ())), preferred_element_type=F32)


def tn(a, b):
    return lax.dot_general(a, b, (((0,), (0,)), ((), ())), preferred_element_type=F32)


def kernel(
    img_hbm, ngain_hbm, proj_hbm, kv_hbm, kgain_hbm, q_hbm, qgain_hbm, hgate_hbm, cot_hbm,
    block_image_hbm, image_len_hbm,
    out,
    ngain, kgain, qgain, hgate, block_image, image_len,
    img, proj, kvall, queries, cot,
    wsend, wsib, wys, wyr, wg,
    projf, kvb, qsend, qin, dqout, dqin, dqs,
    gmade, gsib,
    pgbuf, acc,
    ssem, rsem, lsem,
):
    g = lax.axis_index("group")
    s = lax.axis_index("seq")
    m = lax.axis_index("mp")
    z, x = s // 4, s % 4
    y, c = m // 2, m % 2
    p = gray(z)
    other = 1 - c

    xs = [x, (x + 1) % 4, (x + 3) % 4, (x + 2) % 4]
    zs = [z, gray((p + 1) % 4), gray((p + 3) % 4), gray((p + 2) % 4)]

    sib = (g, s, 2 * y + other)
    ydev = [None] + [(g, s, 2 * ((y + d) % 4) + c) for d in (1, 2, 3)]
    xdev = [(g, z * 4 + xs[1], m), (g, z * 4 + xs[2], m)]
    xfar = (g, z * 4 + xs[3], m)
    zdev = [(g, zs[k] * 4 + x, m) for k in (1, 2, 3)]
    across = (1 - g, s, m)

    def rc(place, src, dst, dev):
        return pltpu.make_async_remote_copy(
            src_ref=src, dst_ref=dst, send_sem=ssem.at[place], recv_sem=rsem.at[place],
            device_id=dev, device_id_type=MESH,
        )

    def send(place, src, dst, dev):
        copy = rc(place, src, dst, dev)
        copy.start()
        return copy

    def left(place, ref):
        rc(place, ref, ref, sib).wait_send()

    def arrived(place, dst):
        rc(place, dst, dst, sib).wait_recv()

    barrier = pltpu.get_barrier_semaphore()
    for dev in ydev[1:]:
        pl.semaphore_signal(barrier, inc=1, device_id=dev, device_id_type=MESH)

    @pl.loop(1, 64)
    def _(k):
        at = (g * 32 + s * 2 + c + k) % 64
        dev = (at // 32, (at // 2) % 16, 2 * y + at % 2)
        pl.semaphore_signal(barrier, inc=1, device_id=dev, device_id_type=MESH)

    local = {}

    def load(name, src, dst):
        copy = pltpu.make_async_copy(src, dst, lsem.at[len(local)])
        local[name] = copy
        return copy

    def strip(par, kind, yy):
        return load(
            ("kv", len(local)),
            kv_hbm.at[:, pl.ds(pl.multiple_of((2 * yy + par) * 256 + kind * 128, 128), 128)],
            kvall.at[par, kind, :, yy * 128:(yy + 1) * 128],
        )

    small = [
        load("ngain", ngain_hbm, ngain),
        load("kgain", kgain_hbm, kgain),
        load("qgain", qgain_hbm, qgain),
        load("hgate", hgate_hbm, hgate),
        load("block_image", block_image_hbm, block_image),
        load("image_len", image_len_hbm, image_len),
    ]
    for copy in small:
        copy.start()
    q_load = load("q", q_hbm, queries)
    q_load.start()
    cot_load = load("cot", cot_hbm, cot)
    cot_load.start()
    proj_load = load("proj", proj_hbm, proj)
    proj_load.start()
    kv_sib = [strip(g, other, yy) for yy in range(4)]
    for copy in kv_sib:
        copy.start()
    kv_own = [strip(g, c, yy) for yy in range(4)]
    for copy in kv_own:
        copy.start()
    img_load = load("img", img_hbm, img)
    kv_rest = [strip(1 - g, kind, yy) for kind in range(2) for yy in range(4)]

    for copy in small:
        copy.wait()
    q_load.wait()
    cot_load.wait()
    gates = [jnp.tanh(jnp.full((1, HD), hgate[h], F32)) for h in range(8)]

    @pl.loop(0, 16, unroll=4)
    def _(i):
        first, last, seen = i * 0, i * 0, i * 0
        for b in range(16):
            hit = (block_image[b] == i).astype(jnp.int32)
            first = first + b * hit * (1 - seen)
            last = last + (b - last) * hit
            seen = seen + hit * (1 - seen)
        zero = jnp.zeros((16, HD), BF16)
        for slot, (at, use) in enumerate(((first, seen > 0), (last, last > first))):
            for h in range(8):
                cols = slice(h * 128, (h + 1) * 128)
                rows = slice((h % 4) * 16, (h % 4 + 1) * 16)
                qsend[i, h // 4, 0, slot, rows, :] = jnp.where(use, queries[at, :, cols], zero)
                grad = (cot[at, :, cols].astype(F32) * gates[h]).astype(BF16)
                qsend[i, h // 4, 1, slot, rows, :] = jnp.where(use, grad, zero)

    pl.semaphore_wait(barrier, 66)

    place_z = g * 4 + z

    def route(which):
        for step, dz in enumerate((2, -2, 1, -1, 0)):
            if dz not in which:
                continue
            to_z = (place_z + dz + 8) % 8

            @pl.when(to_z // 4 == c)
            def _(step=step, dz=dz, to_z=to_z):
                for xrel in (3, 1, 2, 0):
                    owner = (to_z % 4) * 4 + xs[xrel]
                    for part in range(2):
                        place = BASE["route"] + (step * 4 + xrel) * 2 + part
                        src, dst = qsend.at[owner, part], qin.at[s]
                        if dz == 2:
                            src, dst = src.at[0], dst.at[0]
                        if dz == -2:
                            src, dst = src.at[1], dst.at[1]
                        if dz == 0 and xrel == 0:
                            @pl.when(c == part)
                            def _(part=part):
                                qin[s] = qsend[s, part]

                            @pl.when(c != part)
                            def _(place=place, src=src, dst=dst):
                                send(place, src, dst, sib)
                        else:
                            send(place, src, dst, (to_z // 4, owner, 2 * y + part))

    route((1, -1, 0))

    proj_load.wait()
    for copy in kv_sib:
        copy.wait()

    def rows_of(block, r):
        return pl.ds(pl.multiple_of(block * WROWS + r * WHALF, 16), WHALF)

    def wloc(block, r):
        return wg.at[rows_of(block, r), :]

    def block_of(xrel, zrel):
        return zs[zrel] * 4 + xs[xrel]

    def gather(kind, loc):
        zb, xb, xf = BASE[kind + "z"], BASE[kind + "x"], BASE[kind + "xf"]

        def z_own(r):
            ref = loc(block_of(0, 0), r)
            for k in (1, 2, 3):
                send(zb + (k - 1) * 2 + r, ref, ref, zdev[k - 1])

        def x_direct(zrel, r):
            ref = loc(block_of(0, zrel), r)
            for way in (RIGHT, LEFT):
                send(xb + (way * 4 + zrel) * 2 + r, ref, ref, xdev[way])

        def z_in(zrel, r):
            k = (0, 2, 1, 3)[zrel]
            arrived(zb + (k - 1) * 2 + r, loc(block_of(0, zrel), r))
            x_direct(zrel, r)

        def x_first(way, zrel, r):
            xrel = 2 if way == RIGHT else 1
            ref = loc(block_of(xrel, zrel), r)
            arrived(xb + (way * 4 + zrel) * 2 + r, ref)
            if r == way:
                send(xf + way * 4 + zrel, ref, ref, xdev[way])

        def x_second(way, zrel):
            arrived(xf + way * 4 + zrel, loc(block_of(3, zrel), way))

        return z_own, x_direct, z_in, x_first, x_second

    w_z_own, w_x_direct, w_z_in, w_x_first, w_x_second = gather("w", wloc)

    def part_of(q):
        first, size = ((0, 128), (128, 112), (240, 128), (368, 112))[q]
        return slice(first, first + size)

    def share_of(q, kind):
        return jnp.dot(proj[part_of(q), :], kvall[g, kind], preferred_element_type=F32)

    def to_sib(q):
        rows = part_of(q)
        wsend[rows, :] = share_of(q, other).astype(BF16)
        send(BASE["wsib"] + q, wsend.at[rows, :], wsib.at[rows, :], sib)

    def to_y(q):
        rows = part_of(q)
        own = share_of(q, c)
        arrived(BASE["wsib"] + q, wsib.at[rows, :])
        for yy in range(4):
            cols = slice(yy * 128, (yy + 1) * 128)
            wys[yy, rows, :] = (own[:, cols] + wsib[rows, cols].astype(F32)).astype(BF16)
        for d in (2, 1, 3):
            send(
                BASE["wy"] + q * 3 + d - 1,
                wys.at[(y + d) % 4, rows, :],
                wyr.at[d - 1, rows, :],
                ydev[d],
            )

    def own_w(r):
        for q in (2 * r, 2 * r + 1):
            rows = part_of(q)
            total = wys[y, rows, :].astype(F32)
            for d in (1, 2, 3):
                arrived(BASE["wy"] + q * 3 + d - 1, wyr.at[d - 1, rows, :])
                total = total + wyr[d - 1, rows, :].astype(F32)
            start = pl.multiple_of(s * WROWS + rows.start, 16)
            wg[pl.ds(start, rows.stop - rows.start), :] = total.astype(BF16)
        w_z_own(r)
        w_x_direct(0, r)

    to_sib(0)
    for copy in kv_own:
        copy.wait()
    for q in range(4):
        if q < 3:
            to_sib(q + 1)
        to_y(q)
    img_load.start()

    @pl.when(g == 0)
    def _():
        for copy in kv_rest:
            copy.start()
    own_w(0)
    own_w(1)
    route((2, -2))
    for r in (0, 1):
        w_z_in(1, r)
        w_z_in(2, r)

    def route_in(step, dz):
        from_z = (z + 8 - dz) % 4
        for xrel in range(4):
            text = from_z * 4 + (x + (0, 3, 1, 2)[xrel]) % 4
            place = BASE["route"] + (step * 4 + xrel) * 2 + c
            dst = qin.at[text]
            if dz == 2:
                dst = dst.at[0]
            if dz == -2:
                dst = dst.at[1]
            if dz == 0 and xrel == 0:
                @pl.when(c != g)
                def _(place=place, dst=dst):
                    arrived(place, dst)
            else:
                arrived(place, dst)
            if dz != -2:
                wide = qin[text, 0].reshape(128, HD).astype(F32)
                scale = lax.rsqrt(jnp.mean(wide * wide, axis=-1, keepdims=True) + epsilon)
                qin[text, 0] = (wide * scale * qgain[...]).astype(BF16).reshape(2, 64, HD)

    img_load.wait()
    for part in range(4):
        rows = slice(part * 64, (part + 1) * 64)
        lead = img[rows, :VD].astype(F32)
        center = jnp.mean(lead, axis=-1, keepdims=True)
        spread = jnp.mean((lead - center) ** 2, axis=-1, keepdims=True)
        lead = (lead - center) * lax.rsqrt(spread + epsilon)
        for k in range(VD // 128):
            cols = slice(k * 128, (k + 1) * 128)
            img[rows, cols] = (lead[:, cols] * ngain[k:k + 1, :]).astype(BF16)

    for r in (0, 1):
        w_x_first(RIGHT, 0, r)
        w_x_first(LEFT, 0, r)
    for r in (0, 1):
        w_z_in(3, r)
    for zrel in (1, 2, 3):
        for r in (0, 1):
            w_x_first(RIGHT, zrel, r)
            w_x_first(LEFT, zrel, r)
        route_in(zrel + 1, (1, -1, 0)[zrel - 1])
    for zrel in range(4):
        w_x_second(RIGHT, zrel)
        w_x_second(LEFT, zrel)
        cols = pl.ds(pl.multiple_of(zs[zrel] * (4 * WROWS), 128), 4 * WROWS)
        product = jnp.dot(img[:, cols], wg[cols, :], preferred_element_type=F32)
        if zrel == 0:
            projf[...] = product
        else:
            projf[...] += product

    made = projf[...]
    key_scale = lax.rsqrt(jnp.mean(made * made, axis=-1, keepdims=True) + epsilon)
    kvb[c] = jnp.where(c == 0, made * key_scale * kgain[...], made).astype(BF16)

    send(BASE["share"], kvb.at[c], kvb.at[c], sib)

    arrived(BASE["share"], kvb.at[other])

    def give_back(t):
        here = (g == 1) & (c == 1) & (t == s)

        @pl.when(here)
        def _():
            dqin[s, 1] = dqout[t]

        @pl.when(jnp.logical_not(here))
        def _():
            place = BASE["back"] + ((16 + t - s) % 16) * 2 + c
            send(place, dqout.at[t], dqin.at[s, c], (1, t, 2 * y + g))

    gmade[...] = jnp.zeros((2, ROWS, HD), F32)

    def attend(zz, step):
        devices = [zz * 4 + step * 2 + k for k in range(2)]
        low = jnp.concatenate([qin[t, 0].reshape(128, HD) for t in devices], axis=0)
        grad = jnp.concatenate([qin[t, 1].reshape(128, HD) for t in devices], axis=0)
        keys, values = kvb[0], kvb[1]
        scores = nt(keys, low) * INV
        usable = lax.broadcasted_iota(jnp.int32, (ROWS, ROWS), 0) < image_len[s]
        raised = jnp.where(usable, jnp.exp(scores), 0.0)
        over = 1.0 / jnp.sum(raised, axis=0, keepdims=True)
        weight_grads = nt(values, grad)
        inner = jnp.sum(raised * weight_grads, axis=0, keepdims=True) * over
        score_grads = (raised * (over * INV) * (weight_grads - inner)).astype(BF16)
        gmade[0] += jnp.dot(score_grads, low, preferred_element_type=F32)
        gmade[1] += jnp.dot((raised * over).astype(BF16), grad, preferred_element_type=F32)
        back = tn(score_grads, keys).astype(BF16)
        for k, t in enumerate(devices):
            dqout[t] = back[k * 128:(k + 1) * 128].reshape(2, 64, HD)


            @pl.when(g == 0)
            def _(t=t):
                give_back(t)

    for step in range(2):
        attend((z + 0) % 4, step)
    for step in range(2):
        attend((z + 3) % 4, step)
    for step in range(2):
        attend((z + 1) % 4, step)
    route_in(0, 2)
    route_in(1, -2)
    for step in range(2):
        attend((z + 2) % 4, step)

    send(BASE["gsib"], gmade.at[other], gsib, sib)

    arrived(BASE["gsib"], gsib)

    def half(r):
        return slice(r * HALF, (r + 1) * HALF)

    for r in (0, 1):
        total = gmade[c, half(r)] + gsib[half(r)]
        raw = projf[half(r)]
        scale = lax.rsqrt(jnp.mean(raw * raw, axis=-1, keepdims=True) + epsilon)
        scaled = total * kgain[...]
        back = scale * (
            scaled - raw * (scale * scale) * jnp.mean(scaled * raw, axis=-1, keepdims=True)
        )
        pgbuf[g, c, y, half(r)] = jnp.where(c == 0, back, total).astype(BF16)

    @pl.when(g == 1)
    def _():
        copy = send(BASE["pgx"], pgbuf.at[1, c, y], pgbuf.at[1, c, y], across)

        @pl.loop(0, 16)
        def _(far):
            give_back((s + far) % 16)

        for image in range(16):
            for part in range(2):
                place = BASE["back"] + ((16 + s - image) % 16) * 2 + part
                if part == 0:
                    arrived(place, dqin.at[image, part])
                else:
                    @pl.when((c == 0) | (s != image))
                    def _(place=place, image=image):
                        arrived(place, dqin.at[image, 1])

        @pl.loop(0, 16)
        def _(b):
            mine = block_image[b]
            slot = b * 0
            for bb in range(16):
                hit = ((bb < b) & (block_image[bb] == mine)).astype(jnp.int32)
                slot = slot + hit * (1 - slot)
            for part in range(2):
                dqs[part, b] = dqin[mine, part, slot]

        for h in range(8):
            cols = slice(h * 128, (h + 1) * 128)
            rows = slice((h % 4) * 16, (h % 4 + 1) * 16)
            d = dqs[h // 4, :, rows, :].reshape(ROWS, HD).astype(F32) * qgain[...]
            wide = queries[:, :, cols].reshape(ROWS, HD).astype(F32)
            scale = lax.rsqrt(jnp.mean(wide * wide, axis=-1, keepdims=True) + epsilon)
            res = scale * (d - wide * (scale * scale) * jnp.mean(d * wide, axis=-1, keepdims=True))
            out[0, :, cols] = res.astype(BF16)
        copy.wait_send()

    @pl.when(g == 0)
    def _():
        mine = []
        for par in range(2):
            if par == 1:
                arrived(BASE["pgx"], pgbuf.at[1, c, y])
            own = pgbuf.at[par, c, y]
            for d in (2, 1, 3):
                mine.append(send(BASE["pgy"] + par * 3 + d - 1, own, own, ydev[d]))
            mine.append(send(BASE["pgs"] + par * 4, own, own, sib))
            for d in (1, 3, 2):
                ref = pgbuf.at[par, c, (y + 4 - d) % 4]
                arrived(BASE["pgy"] + par * 3 + d - 1, ref)
                mine.append(send(BASE["pgs"] + par * 4 + d, ref, ref, sib))
            if par == 1:
                for copy in kv_rest:
                    copy.wait()

            def term(kind):
                cat = jnp.concatenate([pgbuf[par, kind, yy] for yy in range(4)], axis=1)
                return nt(cat, kvall[par, kind])

            if par == 0:
                acc[...] = term(c)
            else:
                acc[...] += term(c)
            for d in (0, 1, 3, 2):
                arrived(BASE["pgs"] + par * 4 + d, pgbuf.at[par, other, (y + 4 - d) % 4])
            if par == 0:
                acc[...] += term(other)
            else:
                out[0] = (acc[...] + term(other)).astype(BF16)
        for copy in mine:
            copy.wait_send()

    for name, piece in (
        ("wz", wg.at[0:WHALF, :]),
        ("wx", wg.at[0:WHALF, :]),
        ("wxf", wg.at[0:WHALF, :]),
        ("share", kvb.at[0]),
        ("gsib", gsib),
    ):
        for k in range(_sizes[name]):
            left(BASE[name] + k, piece)
    for q in range(4):
        rows = part_of(q)
        left(BASE["wsib"] + q, wsend.at[rows, :])
        for d in (1, 2, 3):
            left(BASE["wy"] + q * 3 + d - 1, wys.at[0, rows, :])

    for step, dz in enumerate((2, -2, 1, -1, 0)):
        to_z = (place_z + dz + 8) % 8

        @pl.when(to_z // 4 == c)
        def _(step=step, dz=dz):
            piece = qsend.at[0, 0, 0] if abs(dz) == 2 else qsend.at[0, 0]
            for xrel in range(4):
                for part in range(2):
                    place = BASE["route"] + (step * 4 + xrel) * 2 + part
                    if dz == 0 and xrel == 0:
                        @pl.when(c != part)
                        def _(place=place):
                            left(place, piece)
                    else:
                        left(place, piece)

    for far in range(16):
        if far == 0:
            @pl.when((g == 0) | (c == 0))
            def _():
                left(BASE["back"] + c, dqout.at[0])
        else:
            left(BASE["back"] + far * 2 + c, dqout.at[0])


def per_device(
    image_states, norm_gain, proj_weight, kv_weight, key_gain, queries, query_gain, head_gate,
    cotangent, block_image, image_len,
):
    anywhere = pl.BlockSpec(memory_space=pl.ANY)
    vmem = pl.BlockSpec(memory_space=pltpu.VMEM)
    V = pltpu.VMEM
    scratch = [
        V((VD // 128, 128), F32),
        V((1, HD), F32),
        V((1, HD), F32),
        pltpu.SMEM((8,), F32),
        pltpu.SMEM((16,), jnp.int32),
        pltpu.SMEM((16,), jnp.int32),
        V((ROWS, VIN), BF16),
        V((WROWS, 1024), BF16),
        V((2, 2, 1024, 512), BF16),
        V((16, 16, 1024), BF16),
        V((16, 16, 1024), BF16),
        V((WROWS, 512), BF16),
        V((WROWS, 512), BF16),
        V((4, WROWS, HD), BF16),
        V((3, WROWS, HD), BF16),
        V((VIN, HD), BF16),
        V((ROWS, HD), F32),
        V((2, ROWS, HD), BF16),
        V((16, 2, 2, 2, 64, HD), BF16),
        V((16, 2, 2, 64, HD), BF16),
        V((16, 2, 64, HD), BF16),
        V((16, 2, 2, 64, HD), BF16),
        V((2, 16, 64, HD), BF16),
        V((2, ROWS, HD), F32),
        V((ROWS, HD), F32),
        V((2, 2, 4, ROWS, HD), BF16),
        V((ROWS, 1024), F32),
        pltpu.SemaphoreType.DMA((PLACES,)),
        pltpu.SemaphoreType.DMA((PLACES,)),
        pltpu.SemaphoreType.DMA((32,)),
    ]
    return pl.pallas_call(
        kernel,
        out_shape=jax.ShapeDtypeStruct((1, ROWS, 1024), BF16),
        in_specs=[anywhere] * 11,
        out_specs=vmem,
        scratch_shapes=scratch,
        compiler_params=pltpu.CompilerParams(
            collective_id=0, has_side_effects=True, vmem_limit_bytes=60 * 2**20
        ),
    )(
        image_states.reshape(ROWS, VIN), norm_gain.reshape(VD // 128, 128), proj_weight, kv_weight,
        key_gain.reshape(1, HD), queries.reshape(16, 16, 1024), query_gain.reshape(1, HD),
        head_gate, cotangent.reshape(16, 16, 1024),
        block_image.reshape(16), image_len,
    )


def solution(mesh):
    placed = (
        P("seq", None, None), P(), P("seq", "mp"), P("mp", None), P(), P("seq", "mp"), P(),
        P("mp"), P("seq", "mp"), P("seq", None), P(),
    )
    return jax.shard_map(
        per_device, mesh=mesh, in_specs=placed, out_specs=P("group", "seq", "mp"), check_vma=False
    )
```

```python
import math

import jax
import jax.numpy as jnp
from jax import lax
from jax.experimental import pallas as pl
from jax.experimental.pallas import tpu as pltpu
from jax.sharding import PartitionSpec as P

MESH = pl.DeviceIdType.MESH
F32, BF16 = jnp.float32, jnp.bfloat16
epsilon = 1e-05

VIN, VD, HD = 7680, 1280, 128
ROWS = 256
WROWS = 480
WHALF = WROWS // 2
HALF = ROWS // 2
INV = 1.0 / math.sqrt(HD)

RIGHT, LEFT = 0, 1

_sizes = dict(
    wsib=4, wy=12, route=40,
    wz=6, wx=16, wxf=8,
    share=1, gsib=1,
    pgx=1, pgy=6, pgs=8, back=32,
)
BASE = {}
_total = 0
for _name, _size in _sizes.items():
    BASE[_name] = _total
    _total += _size
PLACES = _total


def gray(k):
    return k + (k // 2) * (1 - 2 * (k % 2))


def nt(a, b):
    return lax.dot_general(a, b, (((1,), (1,)), ((), ())), preferred_element_type=F32)


def tn(a, b):
    return lax.dot_general(a, b, (((0,), (0,)), ((), ())), preferred_element_type=F32)


def kernel(
    img_hbm, ngain_hbm, proj_hbm, kv_hbm, kgain_hbm, q_hbm, qgain_hbm, hgate_hbm, cot_hbm,
    block_image_hbm, image_len_hbm,
    out,
    ngain, kgain, qgain, hgate, block_image, image_len,
    img, proj, kvall, queries, cot,
    wsend, wsib, wys, wyr, wg,
    projf, kvb, qsend, qin, dqout, dqin, dqs,
    gmade, gsib,
    pgbuf, acc,
    ssem, rsem, lsem,
):
    g = lax.axis_index("group")
    s = lax.axis_index("seq")
    m = lax.axis_index("mp")
    z, x = s // 4, s % 4
    y, c = m // 2, m % 2
    p = gray(z)
    other = 1 - c

    xs = [x, (x + 1) % 4, (x + 3) % 4, (x + 2) % 4]
    zs = [z, gray((p + 1) % 4), gray((p + 3) % 4), gray((p + 2) % 4)]

    sib = (g, s, 2 * y + other)
    ydev = [None] + [(g, s, 2 * ((y + d) % 4) + c) for d in (1, 2, 3)]
    xdev = [(g, z * 4 + xs[1], m), (g, z * 4 + xs[2], m)]
    xfar = (g, z * 4 + xs[3], m)
    zdev = [(g, zs[k] * 4 + x, m) for k in (1, 2, 3)]
    across = (1 - g, s, m)

    def rc(place, src, dst, dev):
        return pltpu.make_async_remote_copy(
            src_ref=src, dst_ref=dst, send_sem=ssem.at[place], recv_sem=rsem.at[place],
            device_id=dev, device_id_type=MESH,
        )

    def send(place, src, dst, dev):
        copy = rc(place, src, dst, dev)
        copy.start()
        return copy

    def left(place, ref):
        rc(place, ref, ref, sib).wait_send()

    def arrived(place, dst):
        rc(place, dst, dst, sib).wait_recv()

    barrier = pltpu.get_barrier_semaphore()
    for dev in ydev[1:]:
        pl.semaphore_signal(barrier, inc=1, device_id=dev, device_id_type=MESH)

    @pl.loop(1, 64)
    def _(k):
        at = (g * 32 + s * 2 + c + k) % 64
        dev = (at // 32, (at // 2) % 16, 2 * y + at % 2)
        pl.semaphore_signal(barrier, inc=1, device_id=dev, device_id_type=MESH)

    local = {}

    def load(name, src, dst):
        copy = pltpu.make_async_copy(src, dst, lsem.at[len(local)])
        local[name] = copy
        return copy

    def strip(par, kind, yy):
        return load(
            ("kv", len(local)),
            kv_hbm.at[:, pl.ds(pl.multiple_of((2 * yy + par) * 256 + kind * 128, 128), 128)],
            kvall.at[par, kind, :, yy * 128:(yy + 1) * 128],
        )

    small = [
        load("ngain", ngain_hbm, ngain),
        load("kgain", kgain_hbm, kgain),
        load("qgain", qgain_hbm, qgain),
        load("hgate", hgate_hbm, hgate),
        load("block_image", block_image_hbm, block_image),
        load("image_len", image_len_hbm, image_len),
    ]
    for copy in small:
        copy.start()
    q_load = load("q", q_hbm, queries)
    q_load.start()
    cot_load = load("cot", cot_hbm, cot)
    cot_load.start()
    proj_load = load("proj", proj_hbm, proj)
    proj_load.start()
    kv_sib = [strip(g, other, yy) for yy in range(4)]
    for copy in kv_sib:
        copy.start()
    kv_own = [strip(g, c, yy) for yy in range(4)]
    for copy in kv_own:
        copy.start()
    img_load = load("img", img_hbm, img)
    kv_rest = [strip(1 - g, kind, yy) for kind in range(2) for yy in range(4)]

    for copy in small:
        copy.wait()
    q_load.wait()
    cot_load.wait()
    gates = [jnp.tanh(jnp.full((1, HD), hgate[h], F32)) for h in range(8)]

    @pl.loop(0, 16, unroll=4)
    def _(i):
        first, last, seen = i * 0, i * 0, i * 0
        for b in range(16):
            hit = (block_image[b] == i).astype(jnp.int32)
            first = first + b * hit * (1 - seen)
            last = last + (b - last) * hit
            seen = seen + hit * (1 - seen)
        zero = jnp.zeros((16, HD), BF16)
        for slot, (at, use) in enumerate(((first, seen > 0), (last, last > first))):
            for h in range(8):
                cols = slice(h * 128, (h + 1) * 128)
                rows = slice((h % 4) * 16, (h % 4 + 1) * 16)
                qsend[i, h // 4, 0, slot, rows, :] = jnp.where(use, queries[at, :, cols], zero)
                grad = (cot[at, :, cols].astype(F32) * gates[h]).astype(BF16)
                qsend[i, h // 4, 1, slot, rows, :] = jnp.where(use, grad, zero)

    pl.semaphore_wait(barrier, 66)

    place_z = g * 4 + z

    def route(which):
        for step, dz in enumerate((2, -2, 1, -1, 0)):
            if dz not in which:
                continue
            to_z = (place_z + dz + 8) % 8

            @pl.when(to_z // 4 == c)
            def _(step=step, dz=dz, to_z=to_z):
                for xrel in (3, 1, 2, 0):
                    owner = (to_z % 4) * 4 + xs[xrel]
                    for part in range(2):
                        place = BASE["route"] + (step * 4 + xrel) * 2 + part
                        src, dst = qsend.at[owner, part], qin.at[s]
                        if dz == 2:
                            src, dst = src.at[0], dst.at[0]
                        if dz == -2:
                            src, dst = src.at[1], dst.at[1]
                        if dz == 0 and xrel == 0:
                            @pl.when(c == part)
                            def _(part=part):
                                qin[s] = qsend[s, part]

                            @pl.when(c != part)
                            def _(place=place, src=src, dst=dst):
                                send(place, src, dst, sib)
                        else:
                            send(place, src, dst, (to_z // 4, owner, 2 * y + part))

    route((1, -1, 0))

    proj_load.wait()
    for copy in kv_sib:
        copy.wait()

    def rows_of(block, r):
        return pl.ds(pl.multiple_of(block * WROWS + r * WHALF, 16), WHALF)

    def wloc(block, r):
        return wg.at[rows_of(block, r), :]

    def block_of(xrel, zrel):
        return zs[zrel] * 4 + xs[xrel]

    def gather(kind, loc):
        zb, xb, xf = BASE[kind + "z"], BASE[kind + "x"], BASE[kind + "xf"]

        def z_own(r):
            ref = loc(block_of(0, 0), r)
            for k in (1, 2, 3):
                send(zb + (k - 1) * 2 + r, ref, ref, zdev[k - 1])

        def x_direct(zrel, r):
            ref = loc(block_of(0, zrel), r)
            for way in (RIGHT, LEFT):
                send(xb + (way * 4 + zrel) * 2 + r, ref, ref, xdev[way])

        def z_in(zrel, r):
            k = (0, 2, 1, 3)[zrel]
            arrived(zb + (k - 1) * 2 + r, loc(block_of(0, zrel), r))
            x_direct(zrel, r)

        def x_first(way, zrel, r):
            xrel = 2 if way == RIGHT else 1
            ref = loc(block_of(xrel, zrel), r)
            arrived(xb + (way * 4 + zrel) * 2 + r, ref)
            if r == way:
                send(xf + way * 4 + zrel, ref, ref, xdev[way])

        def x_second(way, zrel):
            arrived(xf + way * 4 + zrel, loc(block_of(3, zrel), way))

        return z_own, x_direct, z_in, x_first, x_second

    w_z_own, w_x_direct, w_z_in, w_x_first, w_x_second = gather("w", wloc)

    def part_of(q):
        first, size = ((0, 128), (128, 112), (240, 128), (368, 112))[q]
        return slice(first, first + size)

    def share_of(q, kind):
        return jnp.dot(proj[part_of(q), :], kvall[g, kind], preferred_element_type=F32)

    def to_sib(q):
        rows = part_of(q)
        wsend[rows, :] = share_of(q, other).astype(BF16)
        send(BASE["wsib"] + q, wsend.at[rows, :], wsib.at[rows, :], sib)

    def to_y(q):
        rows = part_of(q)
        own = share_of(q, c)
        arrived(BASE["wsib"] + q, wsib.at[rows, :])
        for yy in range(4):
            cols = slice(yy * 128, (yy + 1) * 128)
            wys[yy, rows, :] = (own[:, cols] + wsib[rows, cols].astype(F32)).astype(BF16)
        for d in (2, 1, 3):
            send(
                BASE["wy"] + q * 3 + d - 1,
                wys.at[(y + d) % 4, rows, :],
                wyr.at[d - 1, rows, :],
                ydev[d],
            )

    def own_w(r):
        for q in (2 * r, 2 * r + 1):
            rows = part_of(q)
            total = wys[y, rows, :].astype(F32)
            for d in (1, 2, 3):
                arrived(BASE["wy"] + q * 3 + d - 1, wyr.at[d - 1, rows, :])
                total = total + wyr[d - 1, rows, :].astype(F32)
            start = pl.multiple_of(s * WROWS + rows.start, 16)
            wg[pl.ds(start, rows.stop - rows.start), :] = total.astype(BF16)
        w_z_own(r)
        w_x_direct(0, r)

    to_sib(0)
    for copy in kv_own:
        copy.wait()
    for q in range(4):
        if q < 3:
            to_sib(q + 1)
        to_y(q)
    img_load.start()

    @pl.when(g == 0)
    def _():
        for copy in kv_rest:
            copy.start()
    own_w(0)
    own_w(1)
    route((2, -2))
    for r in (0, 1):
        w_z_in(1, r)
        w_z_in(2, r)

    def route_in(step, dz):
        from_z = (z + 8 - dz) % 4
        for xrel in range(4):
            text = from_z * 4 + (x + (0, 3, 1, 2)[xrel]) % 4
            place = BASE["route"] + (step * 4 + xrel) * 2 + c
            dst = qin.at[text]
            if dz == 2:
                dst = dst.at[0]
            if dz == -2:
                dst = dst.at[1]
            if dz == 0 and xrel == 0:
                @pl.when(c != g)
                def _(place=place, dst=dst):
                    arrived(place, dst)
            else:
                arrived(place, dst)
            if dz != -2:
                wide = qin[text, 0].reshape(128, HD).astype(F32)
                scale = lax.rsqrt(jnp.mean(wide * wide, axis=-1, keepdims=True) + epsilon)
                qin[text, 0] = (wide * scale * qgain[...]).astype(BF16).reshape(2, 64, HD)

    img_load.wait()
    for part in range(4):
        rows = slice(part * 64, (part + 1) * 64)
        lead = img[rows, :VD].astype(F32)
        center = jnp.mean(lead, axis=-1, keepdims=True)
        spread = jnp.mean((lead - center) ** 2, axis=-1, keepdims=True)
        lead = (lead - center) * lax.rsqrt(spread + epsilon)
        for k in range(VD // 128):
            cols = slice(k * 128, (k + 1) * 128)
            img[rows, cols] = (lead[:, cols] * ngain[k:k + 1, :]).astype(BF16)

    for r in (0, 1):
        w_x_first(RIGHT, 0, r)
        w_x_first(LEFT, 0, r)
    for r in (0, 1):
        w_z_in(3, r)
    for zrel in (1, 2, 3):
        for r in (0, 1):
            w_x_first(RIGHT, zrel, r)
            w_x_first(LEFT, zrel, r)
        route_in(zrel + 1, (1, -1, 0)[zrel - 1])
    for zrel in range(4):
        w_x_second(RIGHT, zrel)
        w_x_second(LEFT, zrel)
        cols = pl.ds(pl.multiple_of(zs[zrel] * (4 * WROWS), 128), 4 * WROWS)
        product = jnp.dot(img[:, cols], wg[cols, :], preferred_element_type=F32)
        if zrel == 0:
            projf[...] = product
        else:
            projf[...] += product

    made = projf[...]
    key_scale = lax.rsqrt(jnp.mean(made * made, axis=-1, keepdims=True) + epsilon)
    kvb[c] = jnp.where(c == 0, made * key_scale * kgain[...], made).astype(BF16)

    send(BASE["share"], kvb.at[c], kvb.at[c], sib)

    arrived(BASE["share"], kvb.at[other])

    def give_back(t):
        here = (g == 1) & (c == 1) & (t == s)

        @pl.when(here)
        def _():
            dqin[s, 1] = dqout[t]

        @pl.when(jnp.logical_not(here))
        def _():
            place = BASE["back"] + ((16 + t - s) % 16) * 2 + c
            send(place, dqout.at[t], dqin.at[s, c], (1, t, 2 * y + g))

    gmade[...] = jnp.zeros((2, ROWS, HD), F32)

    def attend(zz, step):
        devices = [zz * 4 + step * 2 + k for k in range(2)]
        low = jnp.concatenate([qin[t, 0].reshape(128, HD) for t in devices], axis=0)
        grad = jnp.concatenate([qin[t, 1].reshape(128, HD) for t in devices], axis=0)
        keys, values = kvb[0], kvb[1]
        scores = nt(keys, low) * INV
        usable = lax.broadcasted_iota(jnp.int32, (ROWS, ROWS), 0) < image_len[s]
        raised = jnp.where(usable, jnp.exp(scores), 0.0)
        over = 1.0 / jnp.sum(raised, axis=0, keepdims=True)
        weight_grads = nt(values, grad)
        inner = jnp.sum(raised * weight_grads, axis=0, keepdims=True) * over
        score_grads = (raised * (over * INV) * (weight_grads - inner)).astype(BF16)
        gmade[0] += jnp.dot(score_grads, low, preferred_element_type=F32)
        gmade[1] += jnp.dot((raised * over).astype(BF16), grad, preferred_element_type=F32)
        back = tn(score_grads, keys).astype(BF16)
        for k, t in enumerate(devices):
            dqout[t] = back[k * 128:(k + 1) * 128].reshape(2, 64, HD)


            @pl.when(g == 0)
            def _(t=t):
                give_back(t)

    for step in range(2):
        attend((z + 0) % 4, step)
    for step in range(2):
        attend((z + 3) % 4, step)
    for step in range(2):
        attend((z + 1) % 4, step)
    route_in(0, 2)
    route_in(1, -2)
    for step in range(2):
        attend((z + 2) % 4, step)

    send(BASE["gsib"], gmade.at[other], gsib, sib)

    arrived(BASE["gsib"], gsib)

    def half(r):
        return slice(r * HALF, (r + 1) * HALF)

    for r in (0, 1):
        total = gmade[c, half(r)] + gsib[half(r)]
        raw = projf[half(r)]
        scale = lax.rsqrt(jnp.mean(raw * raw, axis=-1, keepdims=True) + epsilon)
        scaled = total * kgain[...]
        back = scale * (
            scaled - raw * (scale * scale) * jnp.mean(scaled * raw, axis=-1, keepdims=True)
        )
        pgbuf[g, c, y, half(r)] = jnp.where(c == 0, back, total).astype(BF16)

    @pl.when(g == 1)
    def _():
        copy = send(BASE["pgx"], pgbuf.at[1, c, y], pgbuf.at[1, c, y], across)

        @pl.loop(0, 16)
        def _(far):
            give_back((s + far) % 16)

        for h in range(8):
            wide = queries[:, :, h * 128:(h + 1) * 128].reshape(ROWS, HD).astype(F32)
            scale = lax.rsqrt(jnp.mean(wide * wide, axis=-1, keepdims=True) + epsilon)
            acc[:, h * 128:(h + 1) * 128] = jnp.broadcast_to(scale, (ROWS, HD))

        for image in range(16):
            for part in range(2):
                place = BASE["back"] + ((16 + s - image) % 16) * 2 + part
                if part == 0:
                    arrived(place, dqin.at[image, part])
                else:
                    @pl.when((c == 0) | (s != image))
                    def _(place=place, image=image):
                        arrived(place, dqin.at[image, 1])

        @pl.loop(0, 16)
        def _(b):
            mine = block_image[b]
            slot = b * 0
            for bb in range(16):
                hit = ((bb < b) & (block_image[bb] == mine)).astype(jnp.int32)
                slot = slot + hit * (1 - slot)
            for part in range(2):
                dqs[part, b] = dqin[mine, part, slot]

        for h in range(8):
            cols = slice(h * 128, (h + 1) * 128)
            rows = slice((h % 4) * 16, (h % 4 + 1) * 16)
            d = dqs[h // 4, :, rows, :].reshape(ROWS, HD).astype(F32) * qgain[...]
            wide = queries[:, :, cols].reshape(ROWS, HD).astype(F32)
            scale = acc[:, cols]
            res = scale * (d - wide * (scale * scale) * jnp.mean(d * wide, axis=-1, keepdims=True))
            out[0, :, cols] = res.astype(BF16)
        copy.wait_send()

    @pl.when(g == 0)
    def _():
        mine = []
        for par in range(2):
            if par == 1:
                arrived(BASE["pgx"], pgbuf.at[1, c, y])
            own = pgbuf.at[par, c, y]
            for d in (2, 1, 3):
                mine.append(send(BASE["pgy"] + par * 3 + d - 1, own, own, ydev[d]))
            mine.append(send(BASE["pgs"] + par * 4, own, own, sib))
            for d in (1, 3, 2):
                ref = pgbuf.at[par, c, (y + 4 - d) % 4]
                arrived(BASE["pgy"] + par * 3 + d - 1, ref)
                mine.append(send(BASE["pgs"] + par * 4 + d, ref, ref, sib))
            if par == 1:
                for copy in kv_rest:
                    copy.wait()

            def term(kind):
                cat = jnp.concatenate([pgbuf[par, kind, yy] for yy in range(4)], axis=1)
                return nt(cat, kvall[par, kind])

            if par == 0:
                acc[...] = term(c)
            else:
                acc[...] += term(c)
            for d in (0, 1, 3, 2):
                arrived(BASE["pgs"] + par * 4 + d, pgbuf.at[par, other, (y + 4 - d) % 4])
            if par == 0:
                acc[...] += term(other)
            else:
                out[0] = (acc[...] + term(other)).astype(BF16)
        for copy in mine:
            copy.wait_send()

    for name, piece in (
        ("wz", wg.at[0:WHALF, :]),
        ("wx", wg.at[0:WHALF, :]),
        ("wxf", wg.at[0:WHALF, :]),
        ("share", kvb.at[0]),
        ("gsib", gsib),
    ):
        for k in range(_sizes[name]):
            left(BASE[name] + k, piece)
    for q in range(4):
        rows = part_of(q)
        left(BASE["wsib"] + q, wsend.at[rows, :])
        for d in (1, 2, 3):
            left(BASE["wy"] + q * 3 + d - 1, wys.at[0, rows, :])

    for step, dz in enumerate((2, -2, 1, -1, 0)):
        to_z = (place_z + dz + 8) % 8

        @pl.when(to_z // 4 == c)
        def _(step=step, dz=dz):
            piece = qsend.at[0, 0, 0] if abs(dz) == 2 else qsend.at[0, 0]
            for xrel in range(4):
                for part in range(2):
                    place = BASE["route"] + (step * 4 + xrel) * 2 + part
                    if dz == 0 and xrel == 0:
                        @pl.when(c != part)
                        def _(place=place):
                            left(place, piece)
                    else:
                        left(place, piece)

    for far in range(16):
        if far == 0:
            @pl.when((g == 0) | (c == 0))
            def _():
                left(BASE["back"] + c, dqout.at[0])
        else:
            left(BASE["back"] + far * 2 + c, dqout.at[0])


def per_device(
    image_states, norm_gain, proj_weight, kv_weight, key_gain, queries, query_gain, head_gate,
    cotangent, block_image, image_len,
):
    anywhere = pl.BlockSpec(memory_space=pl.ANY)
    vmem = pl.BlockSpec(memory_space=pltpu.VMEM)
    V = pltpu.VMEM
    scratch = [
        V((VD // 128, 128), F32),
        V((1, HD), F32),
        V((1, HD), F32),
        pltpu.SMEM((8,), F32),
        pltpu.SMEM((16,), jnp.int32),
        pltpu.SMEM((16,), jnp.int32),
        V((ROWS, VIN), BF16),
        V((WROWS, 1024), BF16),
        V((2, 2, 1024, 512), BF16),
        V((16, 16, 1024), BF16),
        V((16, 16, 1024), BF16),
        V((WROWS, 512), BF16),
        V((WROWS, 512), BF16),
        V((4, WROWS, HD), BF16),
        V((3, WROWS, HD), BF16),
        V((VIN, HD), BF16),
        V((ROWS, HD), F32),
        V((2, ROWS, HD), BF16),
        V((16, 2, 2, 2, 64, HD), BF16),
        V((16, 2, 2, 64, HD), BF16),
        V((16, 2, 64, HD), BF16),
        V((16, 2, 2, 64, HD), BF16),
        V((2, 16, 64, HD), BF16),
        V((2, ROWS, HD), F32),
        V((ROWS, HD), F32),
        V((2, 2, 4, ROWS, HD), BF16),
        V((ROWS, 1024), F32),
        pltpu.SemaphoreType.DMA((PLACES,)),
        pltpu.SemaphoreType.DMA((PLACES,)),
        pltpu.SemaphoreType.DMA((32,)),
    ]
    return pl.pallas_call(
        kernel,
        out_shape=jax.ShapeDtypeStruct((1, ROWS, 1024), BF16),
        in_specs=[anywhere] * 11,
        out_specs=vmem,
        scratch_shapes=scratch,
        compiler_params=pltpu.CompilerParams(
            collective_id=0, has_side_effects=True, vmem_limit_bytes=60 * 2**20
        ),
    )(
        image_states.reshape(ROWS, VIN), norm_gain.reshape(VD // 128, 128), proj_weight, kv_weight,
        key_gain.reshape(1, HD), queries.reshape(16, 16, 1024), query_gain.reshape(1, HD),
        head_gate, cotangent.reshape(16, 16, 1024),
        block_image.reshape(16), image_len,
    )


def solution(mesh):
    placed = (
        P("seq", None, None), P(), P("seq", "mp"), P("mp", None), P(), P("seq", "mp"), P(),
        P("mp"), P("seq", "mp"), P("seq", None), P(),
    )
    return jax.shard_map(
        per_device, mesh=mesh, in_specs=placed, out_specs=P("group", "seq", "mp"), check_vma=False
    )
```
